256 devices in a mesh: img: 32 (over z_hi, x, core), cls: 8 (over y, z_lo).
Axes of the slice: x: 4, y: 4, z: 8 (z_hi: 4, z_lo: 2; z = z_hi * 2 + z_lo), core: 2. Of those that a mesh axis runs over, the one named last changes fastest.
Arguments:
- images: bfloat16 [2048, 4608], P('img')
- references: bfloat16 [512, 4608], P('cls')
- shifts: int32 [2048, 2], P('img'), may hold values from -4 to 4
- ctf_groups: int32 [2048], P('img'), may hold values from 0 to 15
- ctf_table: float32 [16, 2304], replicated, may hold values from 0.2 to 1
- noise_var: float32 [32], replicated, may hold values from 4 to 16
Outputs:
- class_sums: float32 [512, 4608], P(('cls', 'img'))
- ctf_sums: float32 [512, 2304], P(('cls', 'img'))
- log_evidence: float32 [2048], P('img')
The draws below stay inside these ranges and needn't reach their ends.
All inputs are finite; a program needn't handle non-finite values.
Results may differ from the reference program's by a relative error of at most 0.013.
Values sent between devices are 32-bit elements; how exact they have to be, the bound alone decides.
No kernel may reach another device: no remote copies, remote signals or barrier semaphores. Data moves between devices by JAX's collectives and lax.ppermute only.
A program may use at most 192 MiB of HBM per device.

```python
import math
import jax
import jax.numpy as jnp
from jax import lax

IMG_DEV = 64
CLASSES = 512
ROT = 36
CYCLES = 32
GROUPS = 16
ANG = 72
BOX = 64
IMAGES = 2048


aligned_count = 16


strengths = (0.5, 1.0, 2.0)


def common_references(key):
    values = jax.random.normal(jax.random.fold_in(key, 101), (CLASSES, 2 * CYCLES * ANG), jnp.float32)
    return 0.25 * jnp.clip(values, -6.0, 6.0)


def common_shifts(key):
    return jax.random.randint(jax.random.fold_in(key, 102), (IMAGES, 2), -4, 5, dtype=jnp.int32)


def rotate_rows(values, amount):
    return jnp.roll(values, amount * 2 * CYCLES, axis=-1)


def unshift(target, moves):
    count = target.shape[0]
    radius = jnp.arange(1, CYCLES + 1, dtype=jnp.float32)
    angle = 2.0 * math.pi * jnp.arange(ANG, dtype=jnp.float32) / ANG
    freq_x = (jnp.cos(angle)[:, None] * radius[None, :]).reshape(-1)
    freq_y = (jnp.sin(angle)[:, None] * radius[None, :]).reshape(-1)
    steps = moves.astype(jnp.float32)
    phase = -2.0 * math.pi / BOX * (steps[:, 0:1] * freq_x[None, :] + steps[:, 1:2] * freq_y[None, :])
    cosine = jnp.cos(phase)
    sine = jnp.sin(phase)
    grid = target.reshape(count, ANG, 2, CYCLES)
    real_part = grid[:, :, 0, :].reshape(count, -1)
    imag_part = grid[:, :, 1, :].reshape(count, -1)
    new_real = (real_part * cosine + imag_part * sine).reshape(count, ANG, CYCLES)
    new_imag = (imag_part * cosine - real_part * sine).reshape(count, ANG, CYCLES)
    return jnp.stack([new_real, new_imag], axis=2).reshape(count, -1)


def drawn_rows(references, moves):
    amplify = 16.0 * 4608.0 / (2 * CYCLES * ANG)
    rows = []
    for index in range(aligned_count):
        turn = index % ROT
        label = 7 * index % CLASSES
        other = (label + 1) % CLASSES
        strength = strengths[index % 3] * amplify
        target = strength * (rotate_rows(references[label:label + 1], 2 * turn) + 0.997 * rotate_rows(references[other:other + 1], 2 * turn))
        rows.append(unshift(target, moves[index:index + 1]))
    return rows


def draw_references(key, part):
    base = common_references(key)
    return base.astype(jnp.bfloat16)


def draw_shifts(key, part):
    base = common_shifts(key)
    return base


def draw_images(key, part):
    references = common_references(key).astype(jnp.bfloat16).astype(jnp.float32)
    moves = common_shifts(key)
    key = jax.random.fold_in(key, 3)
    rows = drawn_rows(references, moves)
    noise = jnp.clip(jax.random.normal(key, (IMAGES, 2 * CYCLES * ANG), jnp.float32), -6.0, 6.0)
    return jnp.concatenate(rows + [noise[aligned_count:]], axis=0).astype(jnp.bfloat16)


def place_ends(values, own_key, low, largest):
    dims = values.shape
    index_at = [jax.random.randint(jax.random.fold_in(own_key, axis), (), 0, dims[axis]) for axis in range(len(dims))]
    values = values.at[tuple(index_at)].set(low)
    longest = dims.index(max(dims))
    index_at[longest] = (index_at[longest] + 1) % dims[longest]
    return values.at[tuple(index_at)].set(largest)


def setup_inputs(seed: int = 0) -> dict:
    arg_keys = jax.random.split(jax.random.key(seed), 7)
    images = draw_images(jax.random.fold_in(arg_keys[6], 71), 0)
    references = draw_references(jax.random.fold_in(arg_keys[6], 71), 0)
    shifts = draw_shifts(jax.random.fold_in(arg_keys[6], 71), 0)
    ctf_groups = place_ends(jax.random.randint(arg_keys[3], (IMAGES,), 0, GROUPS), jax.random.fold_in(arg_keys[3], 1), 0, GROUPS - 1).astype(jnp.int32)
    ctf_table = jnp.clip(jax.random.uniform(arg_keys[4], (GROUPS, CYCLES * ANG), jnp.float32, 0.2, 1.0), 0.2, 1.0)
    noise_var = jnp.clip(jnp.exp(jax.random.uniform(arg_keys[5], (CYCLES,), jnp.float32, math.log(4.0), math.log(16.0))), 4.0, 16.0)
    return dict(images=images, references=references, shifts=shifts, ctf_groups=ctf_groups, ctf_table=ctf_table, noise_var=noise_var)


highest = lax.Precision.HIGHEST


def polar_frequencies():
    radius = jnp.arange(1, CYCLES + 1, dtype=jnp.float32)
    angle = 2.0 * math.pi * jnp.arange(ANG, dtype=jnp.float32) / ANG
    freq_x = (jnp.cos(angle)[:, None] * radius[None, :]).reshape(-1)
    freq_y = (jnp.sin(angle)[:, None] * radius[None, :]).reshape(-1)
    return freq_x, freq_y


def rotate(values, amount, width):
    return jnp.roll(values, amount * width, axis=-1)


def weigh_images(images, shifts, ctf_rows, inverse):
    freq_x, freq_y = polar_frequencies()
    count = images.shape[0]
    grid = images.astype(jnp.float32).reshape(count, ANG, 2, CYCLES)
    real_part = grid[:, :, 0, :].reshape(count, -1)
    imag_part = grid[:, :, 1, :].reshape(count, -1)
    moves = shifts.astype(jnp.float32)
    phase = (-2.0 * math.pi / BOX) * (moves[:, 0:1] * freq_x[None, :] + moves[:, 1:2] * freq_y[None, :])
    cosine = jnp.cos(phase)
    sine = jnp.sin(phase)
    scale = ctf_rows * inverse[None, :]
    shifted_real = ((real_part * cosine - imag_part * sine) * scale).reshape(count, ANG, CYCLES)
    shifted_imag = ((real_part * sine + imag_part * cosine) * scale).reshape(count, ANG, CYCLES)
    joined = jnp.stack([shifted_real, shifted_imag], axis=2).reshape(count, -1)
    return joined.astype(jnp.bfloat16)


def reference(images, references, shifts, ctf_groups, ctf_table, noise_var):
    plane = CYCLES * ANG
    inverse = jnp.tile(1.0 / noise_var, ANG)
    ctf_weight = ctf_table * ctf_table * inverse[None, :]
    ref_values = references.astype(jnp.float32)
    ref_grid = ref_values.reshape(CLASSES, ANG, 2, CYCLES)
    power = jnp.sum(ref_grid * ref_grid, axis=2).reshape(CLASSES, plane)
    rolled_weight = jnp.stack([rotate(ctf_weight, -2 * turn, CYCLES) for turn in range(ROT)])
    penalty = jnp.einsum('rgp,kp->grk', rolled_weight, power, precision=highest)
    batches = IMAGES // IMG_DEV

    def step(carry, inputs):
        numerator, denominator = carry
        batch_images, batch_shifts, batch_groups = inputs
        weighted = weigh_images(batch_images, batch_shifts, ctf_table[batch_groups], inverse).astype(jnp.float32)
        scores = jnp.stack([jnp.dot(weighted, rotate(ref_values, 2 * turn, 2 * CYCLES).T, precision=highest) for turn in range(ROT)], axis=1)
        scores = scores - 0.5 * penalty[batch_groups]
        top = jnp.max(scores, axis=(1, 2))
        expo = jnp.exp(scores - top[:, None, None])
        total = jnp.sum(expo, axis=(1, 2))
        evidence = top + jnp.log(total)
        weights = (expo / total[:, None, None]).astype(jnp.bfloat16)
        weights = lax.optimization_barrier(weights).astype(jnp.float32)
        for turn in range(ROT):
            numerator = numerator + rotate(jnp.dot(weights[:, turn, :].T, weighted, precision=highest), -2 * turn, 2 * CYCLES)
        membership = (batch_groups[:, None] == jnp.arange(GROUPS, dtype=jnp.int32)[None, :]).astype(jnp.float32)
        group_weight = jnp.einsum('irk,ig->rkg', weights, membership, precision=highest)
        denominator = denominator + jnp.einsum('rkg,rgp->kp', group_weight, rolled_weight, precision=highest)
        return (numerator, denominator), evidence

    start = (jnp.zeros((CLASSES, 2 * plane), jnp.float32), jnp.zeros((CLASSES, plane), jnp.float32))
    stacked = (images.reshape(batches, IMG_DEV, 2 * plane), shifts.reshape(batches, IMG_DEV, 2), ctf_groups.reshape(batches, IMG_DEV))
    (numerator, denominator), evidence = lax.scan(step, start, stacked)
    return numerator, denominator, evidence.reshape(-1)
```

```python
import math

import jax
import jax.numpy as jnp
import numpy as np
from jax import lax
from jax.experimental import pallas as pl
from jax.experimental.pallas import tpu as pltpu
from jax.sharding import PartitionSpec as P

ROT = 36
CYCLES = 32
ANG = 72
BOX = 64
GROUPS = 16
IMGS = 64
KDEV = 64
FULL = 2 * ANG * CYCLES
PLANE = ANG * CYCLES
STEP = 4
TURNS = ROT // STEP
ROWS = TURNS * KDEV
COLS = STEP * IMGS
PAIRS = FULL // 256
TILES = PLANE // 256
SENT = FULL + 640

f32 = jnp.float32
bf16 = jnp.bfloat16
NT = (((1,), (1,)), ((), ()))
NN = (((1,), (0,)), ((), ()))


def trig_fit():
    grid = 0.5 * np.cos(np.pi * (np.arange(2000) + 0.5) / 2000)
    square = grid * grid
    cosine = np.polynomial.chebyshev.Chebyshev.fit(square, np.cos(2 * np.pi * grid), 6)
    sine = np.polynomial.chebyshev.Chebyshev.fit(square, np.sin(2 * np.pi * grid) / grid, 6)
    to_power = lambda fit: [float(c) for c in fit.convert(kind=np.polynomial.Polynomial).coef]
    return to_power(cosine), to_power(sine)


COS, SIN = trig_fit()


def horner(coefficients, x):
    value = jnp.full_like(x, coefficients[-1])
    for c in coefficients[-2::-1]:
        value = value * x + c
    return value


def split3(x):
    high = x.astype(bf16)
    rest = x - high.astype(f32)
    middle = rest.astype(bf16)
    low = (rest - middle.astype(f32)).astype(bf16)
    return high, middle, low


def dot(a, b, dims):
    return lax.dot_general(a, b, dims, preferred_element_type=f32)


def block(ref, index, count, width=256):
    index = index % count
    return ref[:, index * width : (index + 1) * width]


def image_tile(w_ref, pair):
    rows = []
    for s in range(STEP):
        first = (2 * pair + s) % (2 * PAIRS)
        if first + 1 < 2 * PAIRS:
            rows.append(w_ref[:, first * 128 : first * 128 + 256])
        else:
            rows.append(jnp.concatenate([w_ref[:, first * 128 :], w_ref[:, :128]], axis=1))
    return jnp.concatenate(rows, axis=0)


def group_rows(groups, rows):
    row = lax.broadcasted_iota(jnp.int32, (rows, COLS), 0)
    column = lax.broadcasted_iota(jnp.int32, (rows, COLS), 1)
    wide = jnp.concatenate([groups] * STEP, axis=1)
    same = ((row // GROUPS) % STEP == column // IMGS) & (row % GROUPS == wide)
    return same


def score_kernel(
    place_ref, images_ref, references_ref, shifts_ref, groups_ref, ctf_ref, noise_ref,
    expo_ref, weighted_ref, stats_ref, weight_ref, refs, power_high, power_low,
):
    lane = lax.broadcasted_iota(jnp.int32, (1, 128), 1)
    lane64 = lax.broadcasted_iota(jnp.int32, (64, 128), 1)
    partner = jnp.bitwise_xor(lane64, 32)
    inverse = jnp.concatenate([1.0 / noise_ref[...]] * 4, axis=1)
    groups = groups_ref[...]

    x, z, core = place_ref[0], place_ref[1], place_ref[2]
    out_row = lax.broadcasted_iota(jnp.int32, (KDEV, KDEV), 0)
    in_row = lax.broadcasted_iota(jnp.int32, (KDEV, KDEV), 1)
    to_core = jnp.where(out_row < 32, 1 - core, core)
    to_x = (x + (out_row // 8) % 4) % 4
    to_z = (z + (out_row // 2) % 4) % 4
    order = (in_row == to_z * 16 + to_x * 4 + to_core * 2 + out_row % 2).astype(f32).astype(bf16)
    for pair in range(PAIRS):
        at = slice(pair * 256, (pair + 1) * 256)
        refs[:, at] = dot(order, references_ref[:, at], NN).astype(bf16)

    for tile in range(PAIRS):
        sums = []
        for chunk in (2 * tile, 2 * tile + 1):
            value = refs[:, chunk * 128 : (chunk + 1) * 128].astype(f32)
            value = value * value
            sums.append(value + jnp.take_along_axis(value, partner, axis=1))
        value = jnp.where(
            lane64 < 64, pltpu.roll(sums[0], 96, 1), pltpu.roll(sums[1], 32, 1)
        )
        high = value.astype(bf16)
        at = slice(tile * 128, (tile + 1) * 128)
        power_high[:, at] = high
        power_low[:, at] = (value - high.astype(f32)).astype(bf16)

    plane = [ctf_ref[:, t * 128 : (t + 1) * 128] for t in range(PAIRS)]
    squared = [v * v * inverse for v in plane]
    swapped = [pltpu.roll(v, 64, 1) for v in squared]
    half = lax.broadcasted_iota(jnp.int32, (GROUPS, 128), 1) < 64
    for s in range(STEP):
        for tile in range(PAIRS):
            first = (tile + s // 2) % PAIRS
            if s % 2 == 0:
                value = squared[first]
            else:
                value = jnp.where(half, swapped[first], swapped[(first + 1) % PAIRS])
            for piece, part in enumerate(split3(value)):
                row = piece * STEP * GROUPS + s * GROUPS
                weight_ref[row : row + GROUPS, tile * 128 : (tile + 1) * 128] = part

    row = lax.broadcasted_iota(jnp.int32, (128, 128), 0)
    column = jnp.concatenate([groups, groups], axis=1)
    hot = jnp.where((row % GROUPS == column) & (row < 3 * GROUPS), 1.0, 0.0)
    hot = jnp.transpose(hot)[:IMGS, : 3 * GROUPS].astype(bf16)
    moves = shifts_ref[...].astype(f32)
    move_x = jnp.broadcast_to(moves[:, 0:1], (IMGS, 128))
    move_y = jnp.broadcast_to(moves[:, 1:2], (IMGS, 128))
    radius = (lane % CYCLES + 1).astype(f32) * jnp.where((lane // CYCLES) % 2 == 0, 1.0, -1.0)
    spread = lax.broadcasted_iota(jnp.int32, (GROUPS, 128), 1)
    spread = (spread // 64) * 32 + spread % 32
    for chunk in range(PAIRS):
        angles = [2.0 * math.pi * a / ANG for a in (2 * chunk, 2 * chunk + 1)]
        freq_x = jnp.where(lane < 64, math.cos(angles[0]), math.cos(angles[1])) * radius
        freq_y = jnp.where(lane < 64, math.sin(angles[0]), math.sin(angles[1])) * radius
        turn = move_x * (freq_x * (1.0 / BOX)) + move_y * (freq_y * (1.0 / BOX))
        turn = turn - jnp.round(turn)
        square = turn * turn
        cosine = horner(COS, square)
        sine = horner(SIN, square) * turn
        for at, sign in ((chunk, 1), (chunk + PAIRS, -1)):
            table = plane[at // 2]
            table = jnp.take_along_axis(table, spread + (at % 2) * 64, axis=1)
            scale = dot(hot, jnp.concatenate(split3(table), axis=0), NN) * inverse
            value = images_ref[:, at * 128 : (at + 1) * 128].astype(f32)
            other = jnp.take_along_axis(value, partner, axis=1) * sine
            value = value * cosine
            value = value + other if sign > 0 else value - other
            weighted_ref[:, at * 128 : (at + 1) * 128] = (value * scale).astype(bf16)

    spun = jnp.concatenate(
        [
            jnp.concatenate(
                [block(power_high, t - turn, TILES) for t in range(TILES)]
                + [block(power_low, t - turn, TILES) for t in range(TILES)],
                axis=1,
            )
            for turn in range(TURNS)
        ],
        axis=0,
    )
    by_group = dot(spun, jnp.concatenate([weight_ref[...], weight_ref[...]], axis=1), NT)
    member = jnp.where(group_rows(groups, 3 * STEP * GROUPS), -0.5, 0.0).astype(bf16)
    scores = sum(dot(piece, member, NN) for piece in split3(by_group))

    spun = jnp.concatenate(
        [
            jnp.concatenate([block(refs, t - 2 * turn, PAIRS) for t in range(PAIRS)], axis=1)
            for turn in range(TURNS)
        ],
        axis=0,
    )
    moved = jnp.concatenate([image_tile(weighted_ref, t) for t in range(PAIRS)], axis=1)
    scores = scores + dot(spun, moved, NT)

    def over_turns(value, join):
        value = join(value[:, :128], value[:, 128:])
        value = jnp.broadcast_to(value, (8, 128))
        return join(value, pltpu.roll(value, 64, 1))

    top = over_turns(jnp.max(scores, axis=0, keepdims=True), jnp.maximum)
    expo = jnp.exp(scores - jnp.concatenate([top, top], axis=1)[:1])
    expo_ref[...] = expo
    total = over_turns(jnp.sum(expo, axis=0, keepdims=True), jnp.add)
    for device in range(stats_ref.shape[0]):
        stats_ref[device, 0:1, :] = top[:1]
        stats_ref[device, 1:2, :] = total[:1]


def sum_kernel(
    stats_ref, mine_ref, expo_ref, weighted_ref, groups_ref, keep_ref, send_ref, evidence_ref,
    scaled, sums,
):
    tops = stats_ref[:, 0, :]
    top = jnp.max(tops, axis=0, keepdims=True)
    total = jnp.sum(stats_ref[:, 1, :] * jnp.exp(tops - top), axis=0, keepdims=True)
    evidence_ref[...] = (top + jnp.log(total))[:, :IMGS]
    factor = jnp.exp(mine_ref[0, 0:1, :] - top) / total
    scaled[...] = (expo_ref[...] * jnp.concatenate([factor, factor], axis=1)).astype(bf16)
    weights = scaled[...]
    for pair in range(PAIRS):
        part = dot(weights, image_tile(weighted_ref, pair), NN)
        for turn in range(TURNS):
            to = (pair - 2 * turn) % PAIRS
            at = slice(to * 256, (to + 1) * 256)
            value = part[turn * KDEV : (turn + 1) * KDEV]
            if pair < 2:
                sums[:, at] = value
            else:
                sums[:, at] += value
    send_ref[:, :FULL] = sums[:32]
    keep_ref[:, :FULL] = sums[32:]
    member = group_rows(groups_ref[...], 2 * STEP * GROUPS).astype(f32).astype(bf16)
    counts = dot(weights, member, NT)
    low = lax.broadcasted_iota(jnp.int32, (KDEV, 128), 1) < 64
    for pair in range((TURNS + 1) // 2):
        first = counts[2 * pair * KDEV : (2 * pair + 1) * KDEV]
        if 2 * pair + 1 < TURNS:
            second = counts[(2 * pair + 1) * KDEV : (2 * pair + 2) * KDEV]
        else:
            second = jnp.zeros_like(first)
        value = jnp.where(low, first, second)
        at = slice(FULL + pair * 128, FULL + (pair + 1) * 128)
        send_ref[:, at] = value[:32]
        keep_ref[:, at] = value[32:]


def last_kernel(a_ref, b_ref, c_ref, d_ref, weight_ref, sums_ref, ctf_ref):
    total = (a_ref[...] + b_ref[...]) + (c_ref[...] + d_ref[...])
    sums_ref[...] = total[:, :FULL]
    counts = jnp.concatenate([total[:, FULL:], jnp.zeros((6, SENT - FULL), f32)], axis=0)
    low = lax.broadcasted_iota(jnp.int32, (8, 128), 1) < 64
    rows = []
    for turn in range(TURNS):
        value = counts[:, (turn // 2) * 128 : (turn // 2 + 1) * 128]
        rows.append(jnp.where(low if turn % 2 == 0 else ~low, value, 0.0))
    counts = jnp.concatenate(rows, axis=0)
    counts = jnp.concatenate([counts] * 3, axis=1)
    size = STEP * GROUPS
    weight = jnp.concatenate(
        [weight_ref[(piece // 2) * size : (piece // 2 + 1) * size, :] for piece in range(6)], axis=0
    )
    spread = sum(dot(piece, weight, NN) for piece in split3(counts))
    for tile in range(TILES):
        value = None
        for turn in range(TURNS):
            source = (tile + turn) % TILES
            term = spread[turn * 8 : (turn + 1) * 8, source * 256 : (source + 1) * 256]
            value = term if value is None else value + term
        ctf_ref[:, tile * 256 : (tile + 1) * 256] = value[:2]


LIMIT = pltpu.CompilerParams(vmem_limit_bytes=48 * 1024 * 1024)


def shape(*dims, dtype=f32):
    return jax.ShapeDtypeStruct(dims, dtype)


def on_device(images, references, shifts, ctf_groups, ctf_table, noise_var):
    cls = lax.axis_size("cls")
    me = lax.axis_index("img")
    core, x, z = me % 2, (me // 2) % 4, me // 8
    groups = ctf_groups.reshape(1, -1)
    vmem = pl.BlockSpec(memory_space=pltpu.VMEM)
    place = jnp.stack([x, z, core]).astype(jnp.int32)
    expo, weighted, stats, weight = pl.pallas_call(
        score_kernel,
        out_shape=(
            shape(ROWS, COLS),
            shape(IMGS, FULL, dtype=bf16),
            shape(cls, 2, 128),
            shape(3 * STEP * GROUPS, PLANE, dtype=bf16),
        ),
        in_specs=[pl.BlockSpec(memory_space=pltpu.SMEM)] + [vmem] * 6,
        scratch_shapes=[
            pltpu.VMEM((KDEV, FULL), bf16),
            pltpu.VMEM((KDEV, PLANE), bf16),
            pltpu.VMEM((KDEV, PLANE), bf16),
        ],
        compiler_params=LIMIT,
        name="scores",
    )(place, images, references, shifts, groups, ctf_table, noise_var.reshape(1, -1))
    gathered = lax.all_to_all(stats, "cls", 0, 0)
    keep, send, evidence = pl.pallas_call(
        sum_kernel,
        out_shape=(shape(KDEV // 2, SENT), shape(KDEV // 2, SENT), shape(1, IMGS)),
        scratch_shapes=[pltpu.VMEM((ROWS, COLS), bf16), pltpu.VMEM((KDEV, FULL), f32)],
        compiler_params=LIMIT,
        name="sums",
    )(gathered, stats, expo, weighted, groups)

    count = lax.axis_size("img")
    over_core = [(i, i ^ 1) for i in range(count)]
    half = keep + lax.ppermute(send, "img", over_core)

    def x_step(d):
        return [(i, (i // 8) * 8 + ((i // 2 + d) % 4) * 2 + i % 2) for i in range(count)]

    def z_step(d):
        return [(i, (i + 8 * d) % count) for i in range(count)]

    quarter = half[:8]
    for d in (1, 2, 3):
        quarter = quarter + lax.ppermute(half[8 * d : 8 * d + 8], "img", x_step(d))
    parts = [quarter[:2]]
    for d in (1, 2, 3):
        parts.append(lax.ppermute(quarter[2 * d : 2 * d + 2], "img", z_step(d)))
    class_sums, ctf_sums = pl.pallas_call(
        last_kernel,
        out_shape=(shape(2, FULL), shape(2, PLANE)),
        compiler_params=LIMIT,
        name="ctf",
    )(*parts, weight)
    return class_sums, ctf_sums, evidence.reshape(-1)


def solution(mesh):
    placed = (P("img", None), P("cls", None), P("img", None), P("img"), P(), P())
    return jax.shard_map(
        on_device,
        mesh=mesh,
        in_specs=placed,
        out_specs=(P(("cls", "img"), None), P(("cls", "img"), None), P("img")),
        check_vma=False,
    )
```

```python
import functools
import math

import jax
import jax.numpy as jnp
import numpy as np
from jax import lax
from jax.experimental import pallas as pl
from jax.experimental.pallas import tpu as pltpu
from jax.sharding import PartitionSpec as P

ROT = 36
CYCLES = 32
ANG = 72
BOX = 64
GROUPS = 16
IMGS = 64
KDEV = 64
FULL = 2 * ANG * CYCLES
PLANE = ANG * CYCLES
STEP = 4
TURNS = ROT // STEP
ROWS = TURNS * KDEV
COLS = STEP * IMGS
PAIRS = FULL // 256
TILES = PLANE // 256
SENT = FULL + 640
WIDE = 12
WIDTH = 256
PARTS = 3

f32 = jnp.float32
bf16 = jnp.bfloat16
NT = (((1,), (1,)), ((), ()))
NN = (((1,), (0,)), ((), ()))


def trig_fit():
    grid = 0.5 * np.cos(np.pi * (np.arange(2000) + 0.5) / 2000)
    square = grid * grid
    cosine = np.polynomial.chebyshev.Chebyshev.fit(square, np.cos(2 * np.pi * grid), 6)
    sine = np.polynomial.chebyshev.Chebyshev.fit(square, np.sin(2 * np.pi * grid) / grid, 6)
    to_power = lambda fit: [float(c) for c in fit.convert(kind=np.polynomial.Polynomial).coef]
    return to_power(cosine), to_power(sine)


COS, SIN = trig_fit()


def horner(coefficients, x):
    value = jnp.full_like(x, coefficients[-1])
    for c in coefficients[-2::-1]:
        value = value * x + c
    return value


def split3(x):
    high = x.astype(bf16)
    rest = x - high.astype(f32)
    middle = rest.astype(bf16)
    low = (rest - middle.astype(f32)).astype(bf16)
    return high, middle, low


def dot(a, b, dims):
    return lax.dot_general(a, b, dims, preferred_element_type=f32)


def block(ref, index, count, width=256):
    index = index % count
    return ref[:, index * width : (index + 1) * width]


def image_tile(w_ref, pair):
    rows = []
    for s in range(STEP):
        first = (2 * pair + s) % (2 * PAIRS)
        if first + 1 < 2 * PAIRS:
            rows.append(w_ref[:, first * 128 : first * 128 + 256])
        else:
            rows.append(jnp.concatenate([w_ref[:, first * 128 :], w_ref[:, :128]], axis=1))
    return jnp.concatenate(rows, axis=0)


def group_rows(groups, rows):
    row = lax.broadcasted_iota(jnp.int32, (rows, COLS), 0)
    column = lax.broadcasted_iota(jnp.int32, (rows, COLS), 1)
    wide = jnp.concatenate([groups] * STEP, axis=1)
    return jnp.where((row & (GROUPS - 1)) == wide, (row >> 4) - (column >> 6), -1)


def score_kernel(
    images_hbm, references_hbm, moves_hbm, groups_hbm, ctf_hbm, noise_hbm,
    expo_ref, weighted_ref, stats_ref, weight_ref, kept_ref,
    images_ref, references_ref, moves_ref, groups_ref, ctf_ref, noise_ref,
    refs, power_high, power_low, wide_high, wide_low, cosines, sines, arrived,
):
    copies = [
        pltpu.make_async_copy(source, target, arrived.at[index])
        for index, (source, target) in enumerate(
            [
                (moves_hbm, moves_ref),
                (groups_hbm, groups_ref),
                (noise_hbm, noise_ref),
                (ctf_hbm, ctf_ref),
                (references_hbm, references_ref),
                (images_hbm, images_ref),
            ]
        )
    ]
    for copy in copies:
        copy.start()

    lane = lax.broadcasted_iota(jnp.int32, (1, 128), 1)
    lane64 = lax.broadcasted_iota(jnp.int32, (64, 128), 1)
    swap = lax.broadcasted_iota(jnp.int32, (256, 256), 0) ^ 32
    swap = swap == lax.broadcasted_iota(jnp.int32, (256, 256), 1)
    swap = jnp.where(swap, 1.0, 0.0).astype(bf16)

    place = lax.axis_index("img")
    core, x, z = lax.rem(place, 2), lax.rem(lax.div(place, 2), 4), lax.div(place, 8)
    out_row = lax.broadcasted_iota(jnp.int32, (KDEV, KDEV), 0)
    in_row = lax.broadcasted_iota(jnp.int32, (KDEV, KDEV), 1)
    to_core = jnp.where(out_row < 32, 1 - core, core)
    to_x = (x + (out_row >> 3)) & 3
    to_z = (z + (out_row >> 1)) & 3
    order = in_row == to_z * 16 + to_x * 4 + to_core * 2 + (out_row & 1)
    order = jnp.where(order, 1.0, 0.0).astype(bf16)

    copies[0].wait()
    copies[1].wait()
    groups = groups_ref[...]
    kept_ref[...] = groups
    row = lax.broadcasted_iota(jnp.int32, (128, 128), 0)
    column = jnp.concatenate([groups, groups], axis=1)
    hot = jnp.where(((row & (GROUPS - 1)) == column) & (row < 3 * GROUPS), 1.0, 0.0)
    moves = jnp.concatenate([moves_ref[...].astype(f32)] * 2, axis=1)
    hot = jnp.where(row == 3 * GROUPS, moves[0:1], hot)
    hot = jnp.where(row == 3 * GROUPS + 1, moves[1:2], hot)
    hot = jnp.transpose(hot)[:IMGS]
    move_x = jnp.broadcast_to(hot[:, 3 * GROUPS : 3 * GROUPS + 1], (IMGS, 128))
    move_y = jnp.broadcast_to(hot[:, 3 * GROUPS + 1 : 3 * GROUPS + 2], (IMGS, 128))
    hot = hot[:, : 3 * GROUPS].astype(bf16)
    radius = ((lane & (CYCLES - 1)) + 1).astype(f32) * jnp.where((lane & CYCLES) == 0, 1.0, -1.0)
    for chunk in range(PAIRS):
        angles = [2.0 * math.pi * a / ANG for a in (2 * chunk, 2 * chunk + 1)]
        freq_x = jnp.where(lane < 64, math.cos(angles[0]), math.cos(angles[1])) * radius
        freq_y = jnp.where(lane < 64, math.sin(angles[0]), math.sin(angles[1])) * radius
        turn = move_x * (freq_x * (1.0 / BOX)) + move_y * (freq_y * (1.0 / BOX))
        turn = turn - jnp.round(turn)
        square = turn * turn
        at = slice(chunk * 128, (chunk + 1) * 128)
        cosines[:, at] = horner(COS, square)
        sines[:, at] = horner(SIN, square) * turn

    copies[2].wait()
    copies[3].wait()
    inverse = jnp.concatenate([1.0 / noise_ref[...]] * 4, axis=1)
    plane = [ctf_ref[:, t * 128 : (t + 1) * 128] for t in range(PAIRS)]
    squared = [v * v * inverse for v in plane]
    swapped = [pltpu.roll(v, 64, 1) for v in squared]
    half = lax.broadcasted_iota(jnp.int32, (GROUPS, 128), 1) < 64
    halfway = [jnp.where(half, swapped[t], swapped[(t + 1) % PAIRS]) for t in range(PAIRS)]
    spare = jnp.zeros((WIDTH - WIDE * GROUPS, PLANE), bf16)
    wide_high[WIDE * GROUPS :, :] = spare
    wide_low[WIDE * GROUPS :, :] = spare
    mixed = lax.broadcasted_iota(jnp.int32, (GROUPS, 128), 1)
    mixed = (mixed & 31) | ((mixed & 32) << 1) | ((mixed & 64) >> 1)
    for odd, values in enumerate((squared, halfway)):
        for tile, value in enumerate(values):
            high = value.astype(bf16)
            low = (value - high.astype(f32)).astype(bf16)
            for s in range(odd, STEP, 2):
                to = (tile - s // 2) % PAIRS
                at = slice(to * 128, (to + 1) * 128)
                weight_ref[s * GROUPS : (s + 1) * GROUPS, at] = high
                weight_ref[(STEP + s) * GROUPS : (STEP + s + 1) * GROUPS, at] = low
            value = jnp.take_along_axis(value, mixed, axis=1)
            high = value.astype(bf16)
            low = (value - high.astype(f32)).astype(bf16)
            for s in range(odd, WIDE, 2):
                to = (tile - s // 2) % PAIRS
                at = slice(to * 128, (to + 1) * 128)
                wide_high[s * GROUPS : (s + 1) * GROUPS, at] = high
                wide_low[s * GROUPS : (s + 1) * GROUPS, at] = low

    copies[4].wait()
    for tile in range(PAIRS):
        at = slice(tile * 256, (tile + 1) * 256)
        value = dot(order, references_ref[:, at], NN)
        refs[:, at] = value.astype(bf16)
        value = value * value
        first, second = value[:, :128], value[:, 128:]
        first = first + pltpu.roll(first, 96, 1)
        second = second + pltpu.roll(second, 32, 1)
        value = jnp.where((lane64 & 32) == 0, first, second)
        high = value.astype(bf16)
        at = slice(tile * 128, (tile + 1) * 128)
        power_high[:, at] = high
        power_low[:, at] = (value - high.astype(f32)).astype(bf16)

    spread = lax.broadcasted_iota(jnp.int32, (GROUPS, 128), 1)
    spread = (spread >> 6) * 32 + (spread & 31)
    def weigh(pair):
        at = slice(pair * 256, (pair + 1) * 256)
        cosine, sine = cosines[:, at], sines[:, at]
        for at, sign in ((pair, 1), (pair + PAIRS // 2, -1)):
            table = plane[at] * inverse
            table = jnp.concatenate(
                [
                    jnp.take_along_axis(table, spread, axis=1),
                    jnp.take_along_axis(table, spread + 64, axis=1),
                ],
                axis=1,
            )
            scale = dot(hot, jnp.concatenate(split3(table), axis=0), NN)
            at = slice(at * 256, (at + 1) * 256)
            value = images_ref[:, at]
            other = dot(value, swap, NN) * sine
            value = value.astype(f32) * cosine
            value = value + other if sign > 0 else value - other
            weighted_ref[:, at] = (value * scale).astype(bf16)

    def spun(ref, count, by, first=0, last=None):
        last = count if last is None else last
        return jnp.concatenate(
            [
                jnp.concatenate(
                    [block(ref, t - turn * by, count) for t in range(first, last)], axis=1
                )
                for turn in range(count // by)
            ],
            axis=0,
        )

    copies[5].wait()
    by_group = None
    for part in range(PARTS):
        first, last = part * TILES // PARTS, (part + 1) * TILES // PARTS
        high = spun(power_high, TILES, 3, first, last)
        low = spun(power_low, TILES, 3, first, last)
        rows = high.shape[0]
        at = slice(first * 256, last * 256)
        both = dot(jnp.concatenate([high, low], axis=0), wide_high[:, at], NT)
        both = (both[:rows] + both[rows:]) + dot(high, wide_low[:, at], NT)
        by_group = both if by_group is None else by_group + both
        for pair in range(first, last):
            weigh(pair)

    pieces = jnp.concatenate(split3(by_group), axis=1)
    penalty = []
    distance = group_rows(groups, WIDTH)
    for first in range(0, WIDE, STEP):
        member = jnp.where(distance == first, -0.5, 0.0).astype(bf16)
        penalty.append(dot(pieces, jnp.concatenate([member] * 3, axis=0), NN))
    count = len(penalty)
    penalty = jnp.concatenate(
        [
            penalty[turn % count][(turn // count) * KDEV : (turn // count + 1) * KDEV]
            for turn in range(TURNS)
        ],
        axis=0,
    )
    moved = jnp.concatenate([image_tile(weighted_ref, t) for t in range(PAIRS)], axis=1)
    scores = dot(spun(refs, PAIRS, 2), moved, NT) + penalty

    def over_turns(value, join):
        value = join(value[:, :128], value[:, 128:])
        value = jnp.broadcast_to(value, (8, 128))
        return join(value, pltpu.roll(value, 64, 1))

    top = over_turns(jnp.max(scores, axis=0, keepdims=True), jnp.maximum)
    expo = jnp.exp(scores - jnp.concatenate([top, top], axis=1)[:1])
    expo_ref[...] = expo
    total = over_turns(jnp.sum(expo, axis=0, keepdims=True), jnp.add)
    for device in range(stats_ref.shape[0]):
        stats_ref[device, 0:1, :] = top[:1]
        stats_ref[device, 1:2, :] = total[:1]


def sum_kernel(first, stats_ref, mine_ref, expo_ref, weighted_ref, groups_ref, out_ref, *rest):
    scaled = rest[-1]
    tops = stats_ref[:, 0, :]
    top = jnp.max(tops, axis=0, keepdims=True)
    total = jnp.sum(stats_ref[:, 1, :] * jnp.exp(tops - top), axis=0, keepdims=True)
    for evidence_ref in rest[:-1]:
        evidence_ref[...] = (top + jnp.log(total))[:, :IMGS]
    factor = jnp.exp(mine_ref[0, 0:1, :] - top) / total
    factor = jnp.concatenate([factor, factor], axis=1)
    half = KDEV // 2
    for turn in range(TURNS):
        source = turn * KDEV + first
        value = expo_ref[source : source + half, :] * factor
        scaled[turn * half : (turn + 1) * half, :] = value.astype(bf16)
    weights = scaled[...]
    for pair in range(PAIRS):
        part = dot(weights, image_tile(weighted_ref, pair), NN)
        for turn in range(TURNS):
            to = (pair - 2 * turn) % PAIRS
            at = slice(to * 256, (to + 1) * 256)
            value = part[turn * half : (turn + 1) * half]
            if pair < 2:
                out_ref[:, at] = value
            else:
                out_ref[:, at] += value
    member = jnp.where(group_rows(groups_ref[...], STEP * GROUPS) == 0, 1.0, 0.0).astype(bf16)
    member = jnp.concatenate([member, member], axis=0)
    counts = dot(weights, member, NT)
    low = lax.broadcasted_iota(jnp.int32, (half, 128), 1) < 64
    for pair in range((TURNS + 1) // 2):
        even = counts[2 * pair * half : (2 * pair + 1) * half]
        if 2 * pair + 1 < TURNS:
            odd = counts[(2 * pair + 1) * half : (2 * pair + 2) * half]
        else:
            odd = jnp.zeros_like(even)
        out_ref[:, FULL + pair * 128 : FULL + (pair + 1) * 128] = jnp.where(low, even, odd)


def last_kernel(a_ref, b_ref, c_ref, d_ref, weight_ref, sums_ref, ctf_ref):
    total = (a_ref[...] + b_ref[...]) + (c_ref[...] + d_ref[...])
    sums_ref[...] = total[:, :FULL]
    counts = jnp.concatenate([total[:, FULL:], jnp.zeros((6, SENT - FULL), f32)], axis=0)
    low = lax.broadcasted_iota(jnp.int32, (8, 128), 1) < 64
    rows = []
    for turn in range(TURNS):
        value = counts[:, (turn // 2) * 128 : (turn // 2 + 1) * 128]
        rows.append(jnp.where(low if turn % 2 == 0 else ~low, value, 0.0))
    counts = jnp.concatenate(rows, axis=0)
    counts = jnp.concatenate([counts] * 2, axis=1)
    high = counts.astype(bf16)
    low = counts - high.astype(f32)
    counts = jnp.concatenate([high.astype(f32), low], axis=0).astype(bf16)
    size = STEP * GROUPS
    weight = jnp.concatenate(
        [weight_ref[(piece // 2) * size : (piece // 2 + 1) * size, :] for piece in range(4)], axis=0
    )
    spread = dot(counts, weight, NN)
    spread = spread[: 8 * TURNS] + spread[8 * TURNS :]
    for tile in range(TILES):
        value = None
        for turn in range(TURNS):
            source = (tile + turn) % TILES
            term = spread[turn * 8 : (turn + 1) * 8, source * 256 : (source + 1) * 256]
            value = term if value is None else value + term
        ctf_ref[:, tile * 256 : (tile + 1) * 256] = value[:2]


LIMIT = pltpu.CompilerParams(vmem_limit_bytes=48 * 1024 * 1024)


def shape(*dims, dtype=f32):
    return jax.ShapeDtypeStruct(dims, dtype)


def on_device(images, references, shifts, ctf_groups, ctf_table, noise_var):
    cls = lax.axis_size("cls")
    groups = ctf_groups.reshape(1, -1)
    inputs = (images, references, shifts.T, groups, ctf_table, noise_var.reshape(1, -1))
    inputs = tuple(pltpu.with_memory_space_constraint(v, pltpu.HBM) for v in inputs)
    expo, weighted, stats, weight, groups = pl.pallas_call(
        score_kernel,
        out_shape=(
            shape(ROWS, COLS),
            shape(IMGS, FULL, dtype=bf16),
            shape(cls, 2, 128),
            shape(2 * STEP * GROUPS, PLANE, dtype=bf16),
            shape(1, IMGS, dtype=jnp.int32),
        ),
        in_specs=[pl.BlockSpec(memory_space=pltpu.HBM)] * 6,
        scratch_shapes=[pltpu.VMEM(value.shape, value.dtype) for value in inputs]
        + [
            pltpu.VMEM((KDEV, FULL), bf16),
            pltpu.VMEM((KDEV, PLANE), bf16),
            pltpu.VMEM((KDEV, PLANE), bf16),
            pltpu.VMEM((WIDTH, PLANE), bf16),
            pltpu.VMEM((WIDTH, PLANE), bf16),
            pltpu.VMEM((IMGS, PLANE), f32),
            pltpu.VMEM((IMGS, PLANE), f32),
            pltpu.SemaphoreType.DMA((6,)),
        ],
        compiler_params=LIMIT,
        name="scores",
    )(*inputs)
    gathered = lax.all_to_all(stats, "cls", 0, 0)
    sums = []
    for first in (0, KDEV // 2):
        evidence = [shape(1, IMGS)] if first else []
        sums += pl.pallas_call(
            functools.partial(sum_kernel, first),
            out_shape=[shape(KDEV // 2, SENT)] + evidence,
            scratch_shapes=[pltpu.VMEM((ROWS // 2, COLS), bf16)],
            compiler_params=LIMIT,
            cost_estimate=pl.CostEstimate(
                flops=ROWS * COLS * FULL, bytes_accessed=2 * ROWS * COLS, transcendentals=0
            ),
            name="sums",
        )(gathered, stats, expo, weighted, groups)
    send, keep, evidence = sums

    count = lax.axis_size("img")
    over_core = [(i, i ^ 1) for i in range(count)]
    half = keep + lax.ppermute(send, "img", over_core)

    def x_step(d):
        return [(i, (i // 8) * 8 + ((i // 2 + d) % 4) * 2 + i % 2) for i in range(count)]

    def z_step(d):
        return [(i, (i + 8 * d) % count) for i in range(count)]

    quarter = half[:8]
    for d in (2, 1, 3):
        quarter = quarter + lax.ppermute(half[8 * d : 8 * d + 8], "img", x_step(d))
    parts = [quarter[:2]]
    for d in (2, 1, 3):
        parts.append(lax.ppermute(quarter[2 * d : 2 * d + 2], "img", z_step(d)))
    class_sums, ctf_sums = pl.pallas_call(
        last_kernel,
        out_shape=(shape(2, FULL), shape(2, PLANE)),
        compiler_params=LIMIT,
        name="ctf",
    )(*parts, weight)
    return class_sums, ctf_sums, evidence.reshape(-1)


def solution(mesh):
    placed = (P("img", None), P("cls", None), P("img", None), P("img"), P(), P())
    return jax.shard_map(
        on_device,
        mesh=mesh,
        in_specs=placed,
        out_specs=(P(("cls", "img"), None), P(("cls", "img"), None), P("img")),
        check_vma=False,
    )
```

```python
import functools
import math

import jax
import jax.numpy as jnp
import numpy as np
from jax import lax
from jax.experimental import pallas as pl
from jax.experimental.pallas import tpu as pltpu
from jax.sharding import PartitionSpec as P

ROT = 36
CYCLES = 32
ANG = 72
BOX = 64
GROUPS = 16
IMGS = 64
KDEV = 64
FULL = 2 * ANG * CYCLES
PLANE = ANG * CYCLES
STEP = 4
TURNS = ROT // STEP
ROWS = TURNS * KDEV
COLS = STEP * IMGS
PAIRS = FULL // 256
TILES = PLANE // 256
SENT = FULL + 640
WIDE = 12
WIDTH = 256
PARTS = 3

f32 = jnp.float32
bf16 = jnp.bfloat16
NT = (((1,), (1,)), ((), ()))
NN = (((1,), (0,)), ((), ()))


def trig_fit():
    grid = 0.5 * np.cos(np.pi * (np.arange(2000) + 0.5) / 2000)
    square = grid * grid
    cosine = np.polynomial.chebyshev.Chebyshev.fit(square, np.cos(2 * np.pi * grid), 6)
    sine = np.polynomial.chebyshev.Chebyshev.fit(square, np.sin(2 * np.pi * grid) / grid, 6)
    to_power = lambda fit: [float(c) for c in fit.convert(kind=np.polynomial.Polynomial).coef]
    return to_power(cosine), to_power(sine)


COS, SIN = trig_fit()


def horner(coefficients, x):
    value = jnp.full_like(x, coefficients[-1])
    for c in coefficients[-2::-1]:
        value = value * x + c
    return value


def split3(x):
    high = x.astype(bf16)
    rest = x - high.astype(f32)
    middle = rest.astype(bf16)
    low = (rest - middle.astype(f32)).astype(bf16)
    return high, middle, low


def dot(a, b, dims):
    return lax.dot_general(a, b, dims, preferred_element_type=f32)


def block(ref, index, count, width=256):
    index = index % count
    return ref[:, index * width : (index + 1) * width]


def image_tile(w_ref, pair):
    rows = []
    for s in range(STEP):
        first = (2 * pair + s) % (2 * PAIRS)
        if first + 1 < 2 * PAIRS:
            rows.append(w_ref[:, first * 128 : first * 128 + 256])
        else:
            rows.append(jnp.concatenate([w_ref[:, first * 128 :], w_ref[:, :128]], axis=1))
    return jnp.concatenate(rows, axis=0)


def group_rows(groups, rows):
    row = lax.broadcasted_iota(jnp.int32, (rows, COLS), 0)
    column = lax.broadcasted_iota(jnp.int32, (rows, COLS), 1)
    wide = jnp.concatenate([groups] * STEP, axis=1)
    return jnp.where((row & (GROUPS - 1)) == wide, (row >> 4) - (column >> 6), -1)


def score_kernel(
    images_hbm, references_hbm, moves_hbm, groups_hbm, ctf_hbm, noise_hbm,
    expo_ref, weighted_ref, stats_ref, weight_ref, kept_ref,
    images_ref, references_ref, moves_ref, groups_ref, ctf_ref, noise_ref,
    refs, power_high, power_low, wide_high, wide_low, cosines, sines, arrived,
):
    copies = [
        pltpu.make_async_copy(source, target, arrived.at[index])
        for index, (source, target) in enumerate(
            [
                (moves_hbm, moves_ref),
                (groups_hbm, groups_ref),
                (noise_hbm, noise_ref),
                (ctf_hbm, ctf_ref),
                (references_hbm, references_ref),
                (images_hbm, images_ref),
            ]
        )
    ]
    for copy in copies:
        copy.start()

    lane = lax.broadcasted_iota(jnp.int32, (1, 128), 1)
    lane64 = lax.broadcasted_iota(jnp.int32, (64, 128), 1)
    swap = lax.broadcasted_iota(jnp.int32, (256, 256), 0) ^ 32
    swap = swap == lax.broadcasted_iota(jnp.int32, (256, 256), 1)
    swap = jnp.where(swap, 1.0, 0.0).astype(bf16)

    place = lax.axis_index("img")
    core, x, z = lax.rem(place, 2), lax.rem(lax.div(place, 2), 4), lax.div(place, 8)
    out_row = lax.broadcasted_iota(jnp.int32, (KDEV, KDEV), 0)
    in_row = lax.broadcasted_iota(jnp.int32, (KDEV, KDEV), 1)
    to_core = jnp.where(out_row < 32, 1 - core, core)
    near, later = out_row >> 3, out_row >> 1
    to_x = (x + jnp.where(to_core == 0, near, later)) & 3
    to_z = (z + jnp.where(to_core == 0, later, near)) & 3
    order = in_row == to_z * 16 + to_x * 4 + to_core * 2 + (out_row & 1)
    order = jnp.where(order, 1.0, 0.0).astype(bf16)

    copies[0].wait()
    copies[1].wait()
    groups = groups_ref[...]
    kept_ref[...] = groups
    row = lax.broadcasted_iota(jnp.int32, (128, 128), 0)
    column = jnp.concatenate([groups, groups], axis=1)
    hot = jnp.where(((row & (GROUPS - 1)) == column) & (row < 3 * GROUPS), 1.0, 0.0)
    moves = jnp.concatenate([moves_ref[...].astype(f32)] * 2, axis=1)
    hot = jnp.where(row == 3 * GROUPS, moves[0:1], hot)
    hot = jnp.where(row == 3 * GROUPS + 1, moves[1:2], hot)
    hot = jnp.transpose(hot)[:IMGS]
    move_x = jnp.broadcast_to(hot[:, 3 * GROUPS : 3 * GROUPS + 1], (IMGS, 128))
    move_y = jnp.broadcast_to(hot[:, 3 * GROUPS + 1 : 3 * GROUPS + 2], (IMGS, 128))
    hot = hot[:, : 3 * GROUPS].astype(bf16)
    radius = ((lane & (CYCLES - 1)) + 1).astype(f32) * jnp.where((lane & CYCLES) == 0, 1.0, -1.0)
    for chunk in range(PAIRS):
        angles = [2.0 * math.pi * a / ANG for a in (2 * chunk, 2 * chunk + 1)]
        freq_x = jnp.where(lane < 64, math.cos(angles[0]), math.cos(angles[1])) * radius
        freq_y = jnp.where(lane < 64, math.sin(angles[0]), math.sin(angles[1])) * radius
        turn = move_x * (freq_x * (1.0 / BOX)) + move_y * (freq_y * (1.0 / BOX))
        turn = turn - jnp.round(turn)
        square = turn * turn
        at = slice(chunk * 128, (chunk + 1) * 128)
        cosines[:, at] = horner(COS, square)
        sines[:, at] = horner(SIN, square) * turn

    copies[2].wait()
    copies[3].wait()
    inverse = jnp.concatenate([1.0 / noise_ref[...]] * 4, axis=1)
    plane = [ctf_ref[:, t * 128 : (t + 1) * 128] for t in range(PAIRS)]
    squared = [v * v * inverse for v in plane]
    swapped = [pltpu.roll(v, 64, 1) for v in squared]
    half = lax.broadcasted_iota(jnp.int32, (GROUPS, 128), 1) < 64
    halfway = [jnp.where(half, swapped[t], swapped[(t + 1) % PAIRS]) for t in range(PAIRS)]
    spare = jnp.zeros((WIDTH - WIDE * GROUPS, PLANE), bf16)
    wide_high[WIDE * GROUPS :, :] = spare
    wide_low[WIDE * GROUPS :, :] = spare
    mixed = lax.broadcasted_iota(jnp.int32, (GROUPS, 128), 1)
    mixed = (mixed & 31) | ((mixed & 32) << 1) | ((mixed & 64) >> 1)
    for odd, values in enumerate((squared, halfway)):
        for tile, value in enumerate(values):
            high = value.astype(bf16)
            low = (value - high.astype(f32)).astype(bf16)
            for s in range(odd, STEP, 2):
                to = (tile - s // 2) % PAIRS
                at = slice(to * 128, (to + 1) * 128)
                weight_ref[s * GROUPS : (s + 1) * GROUPS, at] = high
                weight_ref[(STEP + s) * GROUPS : (STEP + s + 1) * GROUPS, at] = low
            value = jnp.take_along_axis(value, mixed, axis=1)
            high = value.astype(bf16)
            low = (value - high.astype(f32)).astype(bf16)
            for s in range(odd, WIDE, 2):
                to = (tile - s // 2) % PAIRS
                at = slice(to * 128, (to + 1) * 128)
                wide_high[s * GROUPS : (s + 1) * GROUPS, at] = high
                wide_low[s * GROUPS : (s + 1) * GROUPS, at] = low

    copies[4].wait()
    for tile in range(PAIRS):
        at = slice(tile * 256, (tile + 1) * 256)
        value = dot(order, references_ref[:, at], NN)
        refs[:, at] = value.astype(bf16)
        value = value * value
        first, second = value[:, :128], value[:, 128:]
        first = first + pltpu.roll(first, 96, 1)
        second = second + pltpu.roll(second, 32, 1)
        value = jnp.where((lane64 & 32) == 0, first, second)
        high = value.astype(bf16)
        at = slice(tile * 128, (tile + 1) * 128)
        power_high[:, at] = high
        power_low[:, at] = (value - high.astype(f32)).astype(bf16)

    spread = lax.broadcasted_iota(jnp.int32, (GROUPS, 128), 1)
    spread = (spread >> 6) * 32 + (spread & 31)
    def weigh(pair):
        at = slice(pair * 256, (pair + 1) * 256)
        cosine, sine = cosines[:, at], sines[:, at]
        for at, sign in ((pair, 1), (pair + PAIRS // 2, -1)):
            table = plane[at] * inverse
            table = jnp.concatenate(
                [
                    jnp.take_along_axis(table, spread, axis=1),
                    jnp.take_along_axis(table, spread + 64, axis=1),
                ],
                axis=1,
            )
            scale = dot(hot, jnp.concatenate(split3(table), axis=0), NN)
            at = slice(at * 256, (at + 1) * 256)
            value = images_ref[:, at]
            other = dot(value, swap, NN) * sine
            value = value.astype(f32) * cosine
            value = value + other if sign > 0 else value - other
            weighted_ref[:, at] = (value * scale).astype(bf16)

    def spun(ref, count, by, first=0, last=None):
        last = count if last is None else last
        return jnp.concatenate(
            [
                jnp.concatenate(
                    [block(ref, t - turn * by, count) for t in range(first, last)], axis=1
                )
                for turn in range(count // by)
            ],
            axis=0,
        )

    copies[5].wait()
    by_group = None
    for part in range(PARTS):
        first, last = part * TILES // PARTS, (part + 1) * TILES // PARTS
        high = spun(power_high, TILES, 3, first, last)
        low = spun(power_low, TILES, 3, first, last)
        rows = high.shape[0]
        at = slice(first * 256, last * 256)
        both = dot(jnp.concatenate([high, low], axis=0), wide_high[:, at], NT)
        both = (both[:rows] + both[rows:]) + dot(high, wide_low[:, at], NT)
        by_group = both if by_group is None else by_group + both
        for pair in range(first, last):
            weigh(pair)

    pieces = jnp.concatenate(split3(by_group), axis=1)
    penalty = []
    distance = group_rows(groups, WIDTH)
    for first in range(0, WIDE, STEP):
        member = jnp.where(distance == first, -0.5, 0.0).astype(bf16)
        penalty.append(dot(pieces, jnp.concatenate([member] * 3, axis=0), NN))
    count = len(penalty)
    penalty = jnp.concatenate(
        [
            penalty[turn % count][(turn // count) * KDEV : (turn // count + 1) * KDEV]
            for turn in range(TURNS)
        ],
        axis=0,
    )
    moved = jnp.concatenate([image_tile(weighted_ref, t) for t in range(PAIRS)], axis=1)
    scores = dot(spun(refs, PAIRS, 2), moved, NT) + penalty

    def over_turns(value, join):
        value = join(value[:, :128], value[:, 128:])
        value = jnp.broadcast_to(value, (8, 128))
        return join(value, pltpu.roll(value, 64, 1))

    top = over_turns(jnp.max(scores, axis=0, keepdims=True), jnp.maximum)
    expo = jnp.exp(scores - jnp.concatenate([top, top], axis=1)[:1])
    expo_ref[...] = expo
    total = over_turns(jnp.sum(expo, axis=0, keepdims=True), jnp.add)
    for device in range(stats_ref.shape[0]):
        stats_ref[device, 0:1, :] = top[:1]
        stats_ref[device, 1:2, :] = total[:1]


def sum_kernel(first, stats_ref, mine_ref, expo_ref, weighted_ref, groups_ref, out_ref, *rest):
    scaled = rest[-1]
    tops = stats_ref[:, 0, :]
    top = jnp.max(tops, axis=0, keepdims=True)
    total = jnp.sum(stats_ref[:, 1, :] * jnp.exp(tops - top), axis=0, keepdims=True)
    for evidence_ref in rest[:-1]:
        evidence_ref[...] = (top + jnp.log(total))[:, :IMGS]
    factor = jnp.exp(mine_ref[0, 0:1, :] - top) / total
    factor = jnp.concatenate([factor, factor], axis=1)
    half = KDEV // 2
    for turn in range(TURNS):
        source = turn * KDEV + first
        value = expo_ref[source : source + half, :] * factor
        scaled[turn * half : (turn + 1) * half, :] = value.astype(bf16)
    weights = scaled[...]
    for pair in range(PAIRS):
        part = dot(weights, image_tile(weighted_ref, pair), NN)
        for turn in range(TURNS):
            to = (pair - 2 * turn) % PAIRS
            at = slice(to * 256, (to + 1) * 256)
            value = part[turn * half : (turn + 1) * half]
            if pair < 2:
                out_ref[:, at] = value
            else:
                out_ref[:, at] += value
    member = jnp.where(group_rows(groups_ref[...], STEP * GROUPS) == 0, 1.0, 0.0).astype(bf16)
    member = jnp.concatenate([member, member], axis=0)
    counts = dot(weights, member, NT)
    low = lax.broadcasted_iota(jnp.int32, (half, 128), 1) < 64
    for pair in range((TURNS + 1) // 2):
        even = counts[2 * pair * half : (2 * pair + 1) * half]
        if 2 * pair + 1 < TURNS:
            odd = counts[(2 * pair + 1) * half : (2 * pair + 2) * half]
        else:
            odd = jnp.zeros_like(even)
        out_ref[:, FULL + pair * 128 : FULL + (pair + 1) * 128] = jnp.where(low, even, odd)


def last_kernel(a_ref, b_ref, c_ref, d_ref, weight_ref, sums_ref, ctf_ref):
    total = (a_ref[...] + b_ref[...]) + (c_ref[...] + d_ref[...])
    sums_ref[...] = total[:, :FULL]
    counts = jnp.concatenate([total[:, FULL:], jnp.zeros((6, SENT - FULL), f32)], axis=0)
    low = lax.broadcasted_iota(jnp.int32, (8, 128), 1) < 64
    rows = []
    for turn in range(TURNS):
        value = counts[:, (turn // 2) * 128 : (turn // 2 + 1) * 128]
        rows.append(jnp.where(low if turn % 2 == 0 else ~low, value, 0.0))
    counts = jnp.concatenate(rows, axis=0)
    counts = jnp.concatenate([counts] * 2, axis=1)
    high = counts.astype(bf16)
    low = counts - high.astype(f32)
    counts = jnp.concatenate([high.astype(f32), low], axis=0).astype(bf16)
    size = STEP * GROUPS
    weight = jnp.concatenate(
        [weight_ref[(piece // 2) * size : (piece // 2 + 1) * size, :] for piece in range(4)], axis=0
    )
    spread = dot(counts, weight, NN)
    spread = spread[: 8 * TURNS] + spread[8 * TURNS :]
    for tile in range(TILES):
        value = None
        for turn in range(TURNS):
            source = (tile + turn) % TILES
            term = spread[turn * 8 : (turn + 1) * 8, source * 256 : (source + 1) * 256]
            value = term if value is None else value + term
        ctf_ref[:, tile * 256 : (tile + 1) * 256] = value[:2]


LIMIT = pltpu.CompilerParams(vmem_limit_bytes=48 * 1024 * 1024)


def shape(*dims, dtype=f32):
    return jax.ShapeDtypeStruct(dims, dtype)


def on_device(images, references, shifts, ctf_groups, ctf_table, noise_var):
    cls = lax.axis_size("cls")
    groups = ctf_groups.reshape(1, -1)
    inputs = (images, references, shifts.T, groups, ctf_table, noise_var.reshape(1, -1))
    inputs = tuple(pltpu.with_memory_space_constraint(v, pltpu.HBM) for v in inputs)
    expo, weighted, stats, weight, groups = pl.pallas_call(
        score_kernel,
        out_shape=(
            shape(ROWS, COLS),
            shape(IMGS, FULL, dtype=bf16),
            shape(cls, 2, 128),
            shape(2 * STEP * GROUPS, PLANE, dtype=bf16),
            shape(1, IMGS, dtype=jnp.int32),
        ),
        in_specs=[pl.BlockSpec(memory_space=pltpu.HBM)] * 6,
        scratch_shapes=[pltpu.VMEM(value.shape, value.dtype) for value in inputs]
        + [
            pltpu.VMEM((KDEV, FULL), bf16),
            pltpu.VMEM((KDEV, PLANE), bf16),
            pltpu.VMEM((KDEV, PLANE), bf16),
            pltpu.VMEM((WIDTH, PLANE), bf16),
            pltpu.VMEM((WIDTH, PLANE), bf16),
            pltpu.VMEM((IMGS, PLANE), f32),
            pltpu.VMEM((IMGS, PLANE), f32),
            pltpu.SemaphoreType.DMA((6,)),
        ],
        compiler_params=LIMIT,
        name="scores",
    )(*inputs)
    gathered = lax.all_to_all(stats, "cls", 0, 0)
    sums = []
    for first in (0, KDEV // 2):
        evidence = [shape(1, IMGS)] if first else []
        sums += pl.pallas_call(
            functools.partial(sum_kernel, first),
            out_shape=[shape(KDEV // 2, SENT)] + evidence,
            scratch_shapes=[pltpu.VMEM((ROWS // 2, COLS), bf16)],
            compiler_params=LIMIT,
            cost_estimate=pl.CostEstimate(
                flops=ROWS * COLS * FULL, bytes_accessed=2 * ROWS * COLS, transcendentals=0
            ),
            name="sums",
        )(gathered, stats, expo, weighted, groups)
    send, keep, evidence = sums

    count = lax.axis_size("img")
    over_core = [(i, i ^ 1) for i in range(count)]
    half = keep + lax.ppermute(send, "img", over_core)

    def step(value, d, stage):
        pairs = []
        for i in range(count):
            along_x = (i // 8) * 8 + ((i // 2 + d) % 4) * 2 + i % 2
            pairs.append((i, along_x if i % 2 == stage else (i + 8 * d) % count))
        return lax.ppermute(value, "img", pairs)

    quarter = half[:8]
    for d in (2, 1, 3):
        quarter = quarter + step(half[8 * d : 8 * d + 8], d, 0)
    parts = [quarter[:2]]
    for d in (2, 1, 3):
        parts.append(step(quarter[2 * d : 2 * d + 2], d, 1))
    class_sums, ctf_sums = pl.pallas_call(
        last_kernel,
        out_shape=(shape(2, FULL), shape(2, PLANE)),
        compiler_params=LIMIT,
        name="ctf",
    )(*parts, weight)
    return class_sums, ctf_sums, evidence.reshape(-1)


def solution(mesh):
    placed = (P("img", None), P("cls", None), P("img", None), P("img"), P(), P())
    return jax.shard_map(
        on_device,
        mesh=mesh,
        in_specs=placed,
        out_specs=(P(("cls", "img"), None), P(("cls", "img"), None), P("img")),
        check_vma=False,
    )
```

```python
import functools
import math

import jax
import jax.numpy as jnp
import numpy as np
from jax import lax
from jax.experimental import pallas as pl
from jax.experimental.pallas import tpu as pltpu
from jax.sharding import PartitionSpec as P

ROT = 36
CYCLES = 32
ANG = 72
BOX = 64
GROUPS = 16
IMGS = 64
KDEV = 64
FULL = 2 * ANG * CYCLES
PLANE = ANG * CYCLES
STEP = 4
TURNS = ROT // STEP
ROWS = TURNS * KDEV
COLS = STEP * IMGS
PAIRS = FULL // 256
TILES = PLANE // 256
SENT = FULL + 640
WIDE = 12
WIDTH = 256
PARTS = 3

f32 = jnp.float32
bf16 = jnp.bfloat16
NT = (((1,), (1,)), ((), ()))
NN = (((1,), (0,)), ((), ()))


def trig_fit():
    grid = 0.5 * np.cos(np.pi * (np.arange(2000) + 0.5) / 2000)
    square = grid * grid
    cosine = np.polynomial.chebyshev.Chebyshev.fit(square, np.cos(2 * np.pi * grid), 6)
    sine = np.polynomial.chebyshev.Chebyshev.fit(square, np.sin(2 * np.pi * grid) / grid, 6)
    to_power = lambda fit: [float(c) for c in fit.convert(kind=np.polynomial.Polynomial).coef]
    return to_power(cosine), to_power(sine)


COS, SIN = trig_fit()


def horner(coefficients, x):
    value = jnp.full_like(x, coefficients[-1])
    for c in coefficients[-2::-1]:
        value = value * x + c
    return value


def split3(x):
    high = x.astype(bf16)
    rest = x - high.astype(f32)
    middle = rest.astype(bf16)
    low = (rest - middle.astype(f32)).astype(bf16)
    return high, middle, low


def dot(a, b, dims):
    return lax.dot_general(a, b, dims, preferred_element_type=f32)


def block(ref, index, count, width=256):
    index = index % count
    return ref[:, index * width : (index + 1) * width]


def image_tile(w_ref, pair):
    rows = []
    for s in range(STEP):
        first = (2 * pair + s) % (2 * PAIRS)
        if first + 1 < 2 * PAIRS:
            rows.append(w_ref[:, first * 128 : first * 128 + 256])
        else:
            rows.append(jnp.concatenate([w_ref[:, first * 128 :], w_ref[:, :128]], axis=1))
    return jnp.concatenate(rows, axis=0)


def group_rows(groups, rows):
    row = lax.broadcasted_iota(jnp.int32, (rows, COLS), 0)
    column = lax.broadcasted_iota(jnp.int32, (rows, COLS), 1)
    wide = jnp.concatenate([groups] * STEP, axis=1)
    return jnp.where((row & (GROUPS - 1)) == wide, (row >> 4) - (column >> 6), -1)


def score_kernel(
    images_hbm, references_hbm, moves_hbm, groups_hbm, ctf_hbm, noise_hbm,
    expo_ref, weighted_ref, stats_ref, weight_ref, kept_ref,
    images_ref, references_ref, moves_ref, groups_ref, ctf_ref, noise_ref,
    refs, power_high, power_low, wide_high, wide_low, cosines, sines, arrived,
):
    copies = [
        pltpu.make_async_copy(source, target, arrived.at[index])
        for index, (source, target) in enumerate(
            [
                (moves_hbm, moves_ref),
                (groups_hbm, groups_ref),
                (noise_hbm, noise_ref),
                (ctf_hbm, ctf_ref),
                (references_hbm, references_ref),
                (images_hbm, images_ref),
            ]
        )
    ]
    for copy in copies:
        copy.start()

    lane = lax.broadcasted_iota(jnp.int32, (1, 128), 1)
    lane64 = lax.broadcasted_iota(jnp.int32, (64, 128), 1)
    swap = lax.broadcasted_iota(jnp.int32, (256, 256), 0) ^ 32
    swap = swap == lax.broadcasted_iota(jnp.int32, (256, 256), 1)
    swap = jnp.where(swap, 1.0, 0.0).astype(bf16)

    place = lax.axis_index("img")
    core, x, z = lax.rem(place, 2), lax.rem(lax.div(place, 2), 4), lax.div(place, 8)
    out_row = lax.broadcasted_iota(jnp.int32, (KDEV, KDEV), 0)
    in_row = lax.broadcasted_iota(jnp.int32, (KDEV, KDEV), 1)
    to_core = jnp.where(out_row < 32, 1 - core, core)
    near, later = out_row >> 3, out_row >> 1
    to_x = (x + jnp.where(to_core == 0, near, later)) & 3
    to_z = (z + jnp.where(to_core == 0, later, near)) & 3
    order = in_row == to_z * 16 + to_x * 4 + to_core * 2 + (out_row & 1)
    order = jnp.where(order, 1.0, 0.0).astype(bf16)

    copies[0].wait()
    copies[1].wait()
    groups = groups_ref[...]
    kept_ref[...] = groups
    row = lax.broadcasted_iota(jnp.int32, (128, 128), 0)
    column = jnp.concatenate([groups, groups], axis=1)
    hot = jnp.where(((row & (GROUPS - 1)) == column) & (row < 3 * GROUPS), 1.0, 0.0)
    moves = jnp.concatenate([moves_ref[...].astype(f32)] * 2, axis=1)
    hot = jnp.where(row == 3 * GROUPS, moves[0:1], hot)
    hot = jnp.where(row == 3 * GROUPS + 1, moves[1:2], hot)
    hot = jnp.where(row == 3 * GROUPS + 2, column.astype(f32), hot)
    hot = jnp.transpose(hot)[:IMGS]
    group_column = hot[:, 3 * GROUPS + 2 : 3 * GROUPS + 3].astype(jnp.int32)
    move_x = jnp.broadcast_to(hot[:, 3 * GROUPS : 3 * GROUPS + 1], (IMGS, 128))
    move_y = jnp.broadcast_to(hot[:, 3 * GROUPS + 1 : 3 * GROUPS + 2], (IMGS, 128))
    hot = hot[:, : 3 * GROUPS].astype(bf16)
    radius = ((lane & (CYCLES - 1)) + 1).astype(f32) * jnp.where((lane & CYCLES) == 0, 1.0, -1.0)
    for chunk in range(PAIRS):
        angles = [2.0 * math.pi * a / ANG for a in (2 * chunk, 2 * chunk + 1)]
        freq_x = jnp.where(lane < 64, math.cos(angles[0]), math.cos(angles[1])) * radius
        freq_y = jnp.where(lane < 64, math.sin(angles[0]), math.sin(angles[1])) * radius
        turn = move_x * (freq_x * (1.0 / BOX)) + move_y * (freq_y * (1.0 / BOX))
        turn = turn - jnp.round(turn)
        square = turn * turn
        at = slice(chunk * 128, (chunk + 1) * 128)
        cosines[:, at] = horner(COS, square)
        sines[:, at] = horner(SIN, square) * turn

    copies[2].wait()
    copies[3].wait()
    inverse = jnp.concatenate([1.0 / noise_ref[...]] * 4, axis=1)
    plane = [ctf_ref[:, t * 128 : (t + 1) * 128] for t in range(PAIRS)]
    squared = [v * v * inverse for v in plane]
    swapped = [pltpu.roll(v, 64, 1) for v in squared]
    half = lax.broadcasted_iota(jnp.int32, (GROUPS, 128), 1) < 64
    halfway = [jnp.where(half, swapped[t], swapped[(t + 1) % PAIRS]) for t in range(PAIRS)]
    spare = jnp.zeros((WIDTH - WIDE * GROUPS, PLANE), bf16)
    wide_high[WIDE * GROUPS :, :] = spare
    wide_low[WIDE * GROUPS :, :] = spare
    mixed = lax.broadcasted_iota(jnp.int32, (GROUPS, 128), 1)
    mixed = (mixed & 31) | ((mixed & 32) << 1) | ((mixed & 64) >> 1)
    for odd, values in enumerate((squared, halfway)):
        for tile, value in enumerate(values):
            high = value.astype(bf16)
            low = (value - high.astype(f32)).astype(bf16)
            for s in range(odd, STEP, 2):
                to = (tile - s // 2) % PAIRS
                at = slice(to * 128, (to + 1) * 128)
                weight_ref[s * GROUPS : (s + 1) * GROUPS, at] = high
                weight_ref[(STEP + s) * GROUPS : (STEP + s + 1) * GROUPS, at] = low
            value = jnp.take_along_axis(value, mixed, axis=1)
            high = value.astype(bf16)
            low = (value - high.astype(f32)).astype(bf16)
            for s in range(odd, WIDE, 2):
                to = (tile - s // 2) % PAIRS
                at = slice(to * 128, (to + 1) * 128)
                wide_high[s * GROUPS : (s + 1) * GROUPS, at] = high
                wide_low[s * GROUPS : (s + 1) * GROUPS, at] = low

    copies[4].wait()
    for tile in range(PAIRS):
        at = slice(tile * 256, (tile + 1) * 256)
        value = dot(order, references_ref[:, at], NN)
        refs[:, at] = value.astype(bf16)
        value = value * value
        first, second = value[:, :128], value[:, 128:]
        first = first + pltpu.roll(first, 96, 1)
        second = second + pltpu.roll(second, 32, 1)
        value = jnp.where((lane64 & 32) == 0, first, second)
        high = value.astype(bf16)
        at = slice(tile * 128, (tile + 1) * 128)
        power_high[:, at] = high
        power_low[:, at] = (value - high.astype(f32)).astype(bf16)

    spread = lax.broadcasted_iota(jnp.int32, (GROUPS, 128), 1)
    spread = (spread >> 6) * 32 + (spread & 31)
    def weigh(pair):
        at = slice(pair * 256, (pair + 1) * 256)
        cosine, sine = cosines[:, at], sines[:, at]
        for at, sign in ((pair, 1), (pair + PAIRS // 2, -1)):
            table = plane[at] * inverse
            table = jnp.concatenate(
                [
                    jnp.take_along_axis(table, spread, axis=1),
                    jnp.take_along_axis(table, spread + 64, axis=1),
                ],
                axis=1,
            )
            scale = dot(hot, jnp.concatenate(split3(table), axis=0), NN)
            at = slice(at * 256, (at + 1) * 256)
            value = images_ref[:, at]
            other = dot(value, swap, NN) * sine
            value = value.astype(f32) * cosine
            value = value + other if sign > 0 else value - other
            weighted_ref[:, at] = (value * scale).astype(bf16)

    def spun(ref, count, by, first=0, last=None):
        last = count if last is None else last
        return jnp.concatenate(
            [
                jnp.concatenate(
                    [block(ref, t - turn * by, count) for t in range(first, last)], axis=1
                )
                for turn in range(count // by)
            ],
            axis=0,
        )

    copies[5].wait()
    by_group = None
    for part in range(PARTS):
        first, last = part * TILES // PARTS, (part + 1) * TILES // PARTS
        high = spun(power_high, TILES, 3, first, last)
        low = spun(power_low, TILES, 3, first, last)
        rows = high.shape[0]
        at = slice(first * 256, last * 256)
        both = dot(jnp.concatenate([high, low], axis=0), wide_high[:, at], NT)
        both = (both[:rows] + both[rows:]) + dot(high, wide_low[:, at], NT)
        by_group = both if by_group is None else by_group + both
        for pair in range(first, last):
            weigh(pair)

    pieces = jnp.concatenate(split3(by_group), axis=1)
    lane = lax.broadcasted_iota(jnp.int32, (KDEV, pieces.shape[1]), 1)
    third = (lane >> 6) & 3
    penalty = [
        jnp.where(third == turn % 3, pieces[turn // 3 * KDEV : (turn // 3 + 1) * KDEV], 0)
        for turn in range(TURNS)
    ]
    penalty = jnp.concatenate(penalty, axis=0).astype(bf16)
    lane = lax.broadcasted_iota(jnp.int32, (IMGS, WIDTH), 1)
    mine = ((lane & (GROUPS - 1)) == group_column) & (lane < WIDE * GROUPS)
    member = [
        jnp.where(mine & (((lane >> 4) & 3) == s), -0.5, 0.0).astype(bf16) for s in range(STEP)
    ]
    member = jnp.concatenate(member, axis=0)
    moved = [image_tile(weighted_ref, t) for t in range(PAIRS)]
    moved = jnp.concatenate(moved + [member] * 3, axis=1)
    scores = dot(jnp.concatenate([spun(refs, PAIRS, 2), penalty], axis=1), moved, NT)

    def over_turns(value, join):
        value = join(value[:, :128], value[:, 128:])
        value = jnp.broadcast_to(value, (8, 128))
        return join(value, pltpu.roll(value, 64, 1))

    top = over_turns(jnp.max(scores, axis=0, keepdims=True), jnp.maximum)
    expo = jnp.exp(scores - jnp.concatenate([top, top], axis=1)[:1])
    expo_ref[...] = expo
    total = over_turns(jnp.sum(expo, axis=0, keepdims=True), jnp.add)
    for device in range(stats_ref.shape[0]):
        stats_ref[device, 0:1, :] = top[:1]
        stats_ref[device, 1:2, :] = total[:1]


def sum_kernel(first, stats_ref, mine_ref, expo_ref, weighted_ref, groups_ref, out_ref, *rest):
    scaled = rest[-1]
    tops = stats_ref[:, 0, :]
    top = jnp.max(tops, axis=0, keepdims=True)
    total = jnp.sum(stats_ref[:, 1, :] * jnp.exp(tops - top), axis=0, keepdims=True)
    for evidence_ref in rest[:-1]:
        evidence_ref[...] = (top + jnp.log(total))[:, :IMGS]
    factor = jnp.exp(mine_ref[0, 0:1, :] - top) / total
    factor = jnp.concatenate([factor, factor], axis=1)
    half = KDEV // 2
    for turn in range(TURNS):
        source = turn * KDEV + first
        value = expo_ref[source : source + half, :] * factor
        scaled[turn * half : (turn + 1) * half, :] = value.astype(bf16)
    weights = scaled[...]
    for pair in range(PAIRS):
        part = dot(weights, image_tile(weighted_ref, pair), NN)
        for turn in range(TURNS):
            to = (pair - 2 * turn) % PAIRS
            at = slice(to * 256, (to + 1) * 256)
            value = part[turn * half : (turn + 1) * half]
            if pair < 2:
                out_ref[:, at] = value
            else:
                out_ref[:, at] += value
    member = jnp.where(group_rows(groups_ref[...], STEP * GROUPS) == 0, 1.0, 0.0).astype(bf16)
    member = jnp.concatenate([member, member], axis=0)
    counts = dot(weights, member, NT)
    low = lax.broadcasted_iota(jnp.int32, (half, 128), 1) < 64
    for pair in range((TURNS + 1) // 2):
        even = counts[2 * pair * half : (2 * pair + 1) * half]
        if 2 * pair + 1 < TURNS:
            odd = counts[(2 * pair + 1) * half : (2 * pair + 2) * half]
        else:
            odd = jnp.zeros_like(even)
        out_ref[:, FULL + pair * 128 : FULL + (pair + 1) * 128] = jnp.where(low, even, odd)


def last_kernel(a_ref, b_ref, c_ref, d_ref, weight_ref, sums_ref, ctf_ref):
    total = (a_ref[...] + b_ref[...]) + (c_ref[...] + d_ref[...])
    sums_ref[...] = total[:, :FULL]
    counts = jnp.concatenate([total[:, FULL:], jnp.zeros((6, SENT - FULL), f32)], axis=0)
    low = lax.broadcasted_iota(jnp.int32, (8, 128), 1) < 64
    rows = []
    for turn in range(TURNS):
        value = counts[:, (turn // 2) * 128 : (turn // 2 + 1) * 128]
        rows.append(jnp.where(low if turn % 2 == 0 else ~low, value, 0.0))
    counts = jnp.concatenate(rows, axis=0)
    counts = jnp.concatenate([counts] * 2, axis=1)
    high = counts.astype(bf16)
    low = counts - high.astype(f32)
    counts = jnp.concatenate([high.astype(f32), low], axis=0).astype(bf16)
    size = STEP * GROUPS
    weight = jnp.concatenate(
        [weight_ref[(piece // 2) * size : (piece // 2 + 1) * size, :] for piece in range(4)], axis=0
    )
    spread = dot(counts, weight, NN)
    spread = spread[: 8 * TURNS] + spread[8 * TURNS :]
    for tile in range(TILES):
        value = None
        for turn in range(TURNS):
            source = (tile + turn) % TILES
            term = spread[turn * 8 : (turn + 1) * 8, source * 256 : (source + 1) * 256]
            value = term if value is None else value + term
        ctf_ref[:, tile * 256 : (tile + 1) * 256] = value[:2]


LIMIT = pltpu.CompilerParams(vmem_limit_bytes=48 * 1024 * 1024)


def shape(*dims, dtype=f32):
    return jax.ShapeDtypeStruct(dims, dtype)


def on_device(images, references, shifts, ctf_groups, ctf_table, noise_var):
    cls = lax.axis_size("cls")
    groups = ctf_groups.reshape(1, -1)
    inputs = (images, references, shifts.T, groups, ctf_table, noise_var.reshape(1, -1))
    inputs = tuple(pltpu.with_memory_space_constraint(v, pltpu.HBM) for v in inputs)
    expo, weighted, stats, weight, groups = pl.pallas_call(
        score_kernel,
        out_shape=(
            shape(ROWS, COLS),
            shape(IMGS, FULL, dtype=bf16),
            shape(cls, 2, 128),
            shape(2 * STEP * GROUPS, PLANE, dtype=bf16),
            shape(1, IMGS, dtype=jnp.int32),
        ),
        in_specs=[pl.BlockSpec(memory_space=pltpu.HBM)] * 6,
        scratch_shapes=[pltpu.VMEM(value.shape, value.dtype) for value in inputs]
        + [
            pltpu.VMEM((KDEV, FULL), bf16),
            pltpu.VMEM((KDEV, PLANE), bf16),
            pltpu.VMEM((KDEV, PLANE), bf16),
            pltpu.VMEM((WIDTH, PLANE), bf16),
            pltpu.VMEM((WIDTH, PLANE), bf16),
            pltpu.VMEM((IMGS, PLANE), f32),
            pltpu.VMEM((IMGS, PLANE), f32),
            pltpu.SemaphoreType.DMA((6,)),
        ],
        compiler_params=LIMIT,
        name="scores",
    )(*inputs)
    gathered = lax.all_to_all(stats, "cls", 0, 0)
    sums = []
    for first in (0, KDEV // 2):
        evidence = [shape(1, IMGS)] if first else []
        sums += pl.pallas_call(
            functools.partial(sum_kernel, first),
            out_shape=[shape(KDEV // 2, SENT)] + evidence,
            scratch_shapes=[pltpu.VMEM((ROWS // 2, COLS), bf16)],
            compiler_params=LIMIT,
            cost_estimate=pl.CostEstimate(
                flops=ROWS * COLS * FULL, bytes_accessed=2 * ROWS * COLS, transcendentals=0
            ),
            name="sums",
        )(gathered, stats, expo, weighted, groups)
    send, keep, evidence = sums

    count = lax.axis_size("img")
    over_core = [(i, i ^ 1) for i in range(count)]
    half = keep + lax.ppermute(send, "img", over_core)

    def step(value, d, stage):
        pairs = []
        for i in range(count):
            along_x = (i // 8) * 8 + ((i // 2 + d) % 4) * 2 + i % 2
            pairs.append((i, along_x if i % 2 == stage else (i + 8 * d) % count))
        return lax.ppermute(value, "img", pairs)

    quarter = half[:8]
    for d in (2, 1, 3):
        quarter = quarter + step(half[8 * d : 8 * d + 8], d, 0)
    parts = [quarter[:2]]
    for d in (2, 1, 3):
        parts.append(step(quarter[2 * d : 2 * d + 2], d, 1))
    class_sums, ctf_sums = pl.pallas_call(
        last_kernel,
        out_shape=(shape(2, FULL), shape(2, PLANE)),
        compiler_params=LIMIT,
        name="ctf",
    )(*parts, weight)
    return class_sums, ctf_sums, evidence.reshape(-1)


def solution(mesh):
    placed = (P("img", None), P("cls", None), P("img", None), P("img"), P(), P())
    return jax.shard_map(
        on_device,
        mesh=mesh,
        in_specs=placed,
        out_specs=(P(("cls", "img"), None), P(("cls", "img"), None), P("img")),
        check_vma=False,
    )
```

```python
import functools
import math

import jax
import jax.numpy as jnp
import numpy as np
from jax import lax
from jax.experimental import pallas as pl
from jax.experimental.pallas import tpu as pltpu
from jax.sharding import PartitionSpec as P

ROT = 36
CYCLES = 32
ANG = 72
BOX = 64
GROUPS = 16
IMGS = 64
KDEV = 64
FULL = 2 * ANG * CYCLES
PLANE = ANG * CYCLES
STEP = 4
TURNS = ROT // STEP
ROWS = TURNS * KDEV
COLS = STEP * IMGS
PAIRS = FULL // 256
TILES = PLANE // 256
SENT = FULL + 640
WIDE = 12
WIDTH = 256
PARTS = 3

f32 = jnp.float32
bf16 = jnp.bfloat16
NT = (((1,), (1,)), ((), ()))
NN = (((1,), (0,)), ((), ()))


def trig_fit():
    grid = 0.5 * np.cos(np.pi * (np.arange(2000) + 0.5) / 2000)
    square = grid * grid
    cosine = np.polynomial.chebyshev.Chebyshev.fit(square, np.cos(2 * np.pi * grid), 6)
    sine = np.polynomial.chebyshev.Chebyshev.fit(square, np.sin(2 * np.pi * grid) / grid, 6)
    to_power = lambda fit: [float(c) for c in fit.convert(kind=np.polynomial.Polynomial).coef]
    return to_power(cosine), to_power(sine)


COS, SIN = trig_fit()


def horner(coefficients, x):
    value = jnp.full_like(x, coefficients[-1])
    for c in coefficients[-2::-1]:
        value = value * x + c
    return value


def split3(x):
    high = x.astype(bf16)
    rest = x - high.astype(f32)
    middle = rest.astype(bf16)
    low = (rest - middle.astype(f32)).astype(bf16)
    return high, middle, low


def dot(a, b, dims):
    return lax.dot_general(a, b, dims, preferred_element_type=f32)


def block(ref, index, count, width=256):
    index = index % count
    return ref[:, index * width : (index + 1) * width]


def image_tile(w_ref, pair):
    rows = []
    for s in range(STEP):
        first = (2 * pair + s) % (2 * PAIRS)
        if first + 1 < 2 * PAIRS:
            rows.append(w_ref[:, first * 128 : first * 128 + 256])
        else:
            rows.append(jnp.concatenate([w_ref[:, first * 128 :], w_ref[:, :128]], axis=1))
    return jnp.concatenate(rows, axis=0)


def group_rows(groups, rows):
    row = lax.broadcasted_iota(jnp.int32, (rows, COLS), 0)
    column = lax.broadcasted_iota(jnp.int32, (rows, COLS), 1)
    wide = jnp.concatenate([groups] * STEP, axis=1)
    return jnp.where((row & (GROUPS - 1)) == wide, (row >> 4) - (column >> 6), -1)


def score_kernel(
    images_hbm, references_hbm, moves_hbm, groups_hbm, ctf_hbm, noise_hbm,
    expo_ref, weighted_ref, stats_ref, weight_ref, kept_ref,
    images_ref, references_ref, moves_ref, groups_ref, ctf_ref, noise_ref,
    refs, power_high, power_low, wide_high, wide_low, cosines, sines, arrived,
):
    copies = [
        pltpu.make_async_copy(source, target, arrived.at[index])
        for index, (source, target) in enumerate(
            [
                (moves_hbm, moves_ref),
                (groups_hbm, groups_ref),
                (noise_hbm, noise_ref),
                (ctf_hbm, ctf_ref),
                (references_hbm, references_ref),
                (images_hbm, images_ref),
            ]
        )
    ]
    for copy in copies:
        copy.start()

    lane = lax.broadcasted_iota(jnp.int32, (1, 128), 1)
    lane64 = lax.broadcasted_iota(jnp.int32, (64, 128), 1)
    swap = lax.broadcasted_iota(jnp.int32, (256, 256), 0) ^ 32
    swap = swap == lax.broadcasted_iota(jnp.int32, (256, 256), 1)
    swap = jnp.where(swap, 1.0, 0.0).astype(bf16)

    place = lax.axis_index("img")
    core, x, z = lax.rem(place, 2), lax.rem(lax.div(place, 2), 4), lax.div(place, 8)
    out_row = lax.broadcasted_iota(jnp.int32, (KDEV, KDEV), 0)
    in_row = lax.broadcasted_iota(jnp.int32, (KDEV, KDEV), 1)
    to_core = jnp.where(out_row < 32, 1 - core, core)
    near, later = out_row >> 3, out_row >> 1
    to_x = x ^ (jnp.where(to_core == 0, near, later) & 3)
    to_z = z ^ (jnp.where(to_core == 0, later, near) & 3)
    order = in_row == to_z * 16 + to_x * 4 + to_core * 2 + (out_row & 1)
    order = jnp.where(order, 1.0, 0.0).astype(bf16)

    copies[0].wait()
    copies[1].wait()
    groups = groups_ref[...]
    kept_ref[...] = groups
    row = lax.broadcasted_iota(jnp.int32, (128, 128), 0)
    column = jnp.concatenate([groups, groups], axis=1)
    hot = jnp.where(((row & (GROUPS - 1)) == column) & (row < 3 * GROUPS), 1.0, 0.0)
    moves = jnp.concatenate([moves_ref[...].astype(f32)] * 2, axis=1)
    hot = jnp.where(row == 3 * GROUPS, moves[0:1], hot)
    hot = jnp.where(row == 3 * GROUPS + 1, moves[1:2], hot)
    hot = jnp.where(row == 3 * GROUPS + 2, column.astype(f32), hot)
    hot = jnp.transpose(hot)[:IMGS]
    group_column = hot[:, 3 * GROUPS + 2 : 3 * GROUPS + 3].astype(jnp.int32)
    move_x = jnp.broadcast_to(hot[:, 3 * GROUPS : 3 * GROUPS + 1], (IMGS, 128))
    move_y = jnp.broadcast_to(hot[:, 3 * GROUPS + 1 : 3 * GROUPS + 2], (IMGS, 128))
    hot = hot[:, : 3 * GROUPS].astype(bf16)
    radius = ((lane & (CYCLES - 1)) + 1).astype(f32) * jnp.where((lane & CYCLES) == 0, 1.0, -1.0)
    for chunk in range(PAIRS):
        angles = [2.0 * math.pi * a / ANG for a in (2 * chunk, 2 * chunk + 1)]
        freq_x = jnp.where(lane < 64, math.cos(angles[0]), math.cos(angles[1])) * radius
        freq_y = jnp.where(lane < 64, math.sin(angles[0]), math.sin(angles[1])) * radius
        turn = move_x * (freq_x * (1.0 / BOX)) + move_y * (freq_y * (1.0 / BOX))
        turn = turn - jnp.round(turn)
        square = turn * turn
        at = slice(chunk * 128, (chunk + 1) * 128)
        cosines[:, at] = horner(COS, square)
        sines[:, at] = horner(SIN, square) * turn

    copies[2].wait()
    copies[3].wait()
    inverse = jnp.concatenate([1.0 / noise_ref[...]] * 4, axis=1)
    plane = [ctf_ref[:, t * 128 : (t + 1) * 128] for t in range(PAIRS)]
    squared = [v * v * inverse for v in plane]
    swapped = [pltpu.roll(v, 64, 1) for v in squared]
    half = lax.broadcasted_iota(jnp.int32, (GROUPS, 128), 1) < 64
    halfway = [jnp.where(half, swapped[t], swapped[(t + 1) % PAIRS]) for t in range(PAIRS)]
    spare = jnp.zeros((WIDTH - WIDE * GROUPS, PLANE), bf16)
    wide_high[WIDE * GROUPS :, :] = spare
    wide_low[WIDE * GROUPS :, :] = spare
    mixed = lax.broadcasted_iota(jnp.int32, (GROUPS, 128), 1)
    mixed = (mixed & 31) | ((mixed & 32) << 1) | ((mixed & 64) >> 1)
    for odd, values in enumerate((squared, halfway)):
        for tile, value in enumerate(values):
            high = value.astype(bf16)
            low = (value - high.astype(f32)).astype(bf16)
            for s in range(odd, STEP, 2):
                to = (tile - s // 2) % PAIRS
                at = slice(to * 128, (to + 1) * 128)
                weight_ref[s * GROUPS : (s + 1) * GROUPS, at] = high
                weight_ref[(STEP + s) * GROUPS : (STEP + s + 1) * GROUPS, at] = low
            value = jnp.take_along_axis(value, mixed, axis=1)
            high = value.astype(bf16)
            low = (value - high.astype(f32)).astype(bf16)
            for s in range(odd, WIDE, 2):
                to = (tile - s // 2) % PAIRS
                at = slice(to * 128, (to + 1) * 128)
                wide_high[s * GROUPS : (s + 1) * GROUPS, at] = high
                wide_low[s * GROUPS : (s + 1) * GROUPS, at] = low

    copies[4].wait()
    for tile in range(PAIRS):
        at = slice(tile * 256, (tile + 1) * 256)
        value = dot(order, references_ref[:, at], NN)
        refs[:, at] = value.astype(bf16)
        value = value * value
        first, second = value[:, :128], value[:, 128:]
        first = first + pltpu.roll(first, 96, 1)
        second = second + pltpu.roll(second, 32, 1)
        value = jnp.where((lane64 & 32) == 0, first, second)
        high = value.astype(bf16)
        at = slice(tile * 128, (tile + 1) * 128)
        power_high[:, at] = high
        power_low[:, at] = (value - high.astype(f32)).astype(bf16)

    spread = lax.broadcasted_iota(jnp.int32, (GROUPS, 128), 1)
    spread = (spread >> 6) * 32 + (spread & 31)
    def weigh(pair):
        at = slice(pair * 256, (pair + 1) * 256)
        cosine, sine = cosines[:, at], sines[:, at]
        for at, sign in ((pair, 1), (pair + PAIRS // 2, -1)):
            table = plane[at] * inverse
            table = jnp.concatenate(
                [
                    jnp.take_along_axis(table, spread, axis=1),
                    jnp.take_along_axis(table, spread + 64, axis=1),
                ],
                axis=1,
            )
            scale = dot(hot, jnp.concatenate(split3(table), axis=0), NN)
            at = slice(at * 256, (at + 1) * 256)
            value = images_ref[:, at]
            other = dot(value, swap, NN) * sine
            value = value.astype(f32) * cosine
            value = value + other if sign > 0 else value - other
            weighted_ref[:, at] = (value * scale).astype(bf16)

    def spun(ref, count, by, first=0, last=None):
        last = count if last is None else last
        return jnp.concatenate(
            [
                jnp.concatenate(
                    [block(ref, t - turn * by, count) for t in range(first, last)], axis=1
                )
                for turn in range(count // by)
            ],
            axis=0,
        )

    copies[5].wait()
    by_group = None
    for part in range(PARTS):
        first, last = part * TILES // PARTS, (part + 1) * TILES // PARTS
        high = spun(power_high, TILES, 3, first, last)
        low = spun(power_low, TILES, 3, first, last)
        rows = high.shape[0]
        at = slice(first * 256, last * 256)
        both = dot(jnp.concatenate([high, low], axis=0), wide_high[:, at], NT)
        both = (both[:rows] + both[rows:]) + dot(high, wide_low[:, at], NT)
        by_group = both if by_group is None else by_group + both
        for pair in range(first, last):
            weigh(pair)

    pieces = jnp.concatenate(split3(by_group), axis=1)
    lane = lax.broadcasted_iota(jnp.int32, (KDEV, pieces.shape[1]), 1)
    third = (lane >> 6) & 3
    penalty = [
        jnp.where(third == turn % 3, pieces[turn // 3 * KDEV : (turn // 3 + 1) * KDEV], 0)
        for turn in range(TURNS)
    ]
    penalty = jnp.concatenate(penalty, axis=0).astype(bf16)
    lane = lax.broadcasted_iota(jnp.int32, (IMGS, WIDTH), 1)
    mine = ((lane & (GROUPS - 1)) == group_column) & (lane < WIDE * GROUPS)
    member = [
        jnp.where(mine & (((lane >> 4) & 3) == s), -0.5, 0.0).astype(bf16) for s in range(STEP)
    ]
    member = jnp.concatenate(member, axis=0)
    moved = [image_tile(weighted_ref, t) for t in range(PAIRS)]
    moved = jnp.concatenate(moved + [member] * 3, axis=1)
    scores = dot(jnp.concatenate([spun(refs, PAIRS, 2), penalty], axis=1), moved, NT)

    def over_turns(value, join):
        value = join(value[:, :128], value[:, 128:])
        value = jnp.broadcast_to(value, (8, 128))
        return join(value, pltpu.roll(value, 64, 1))

    top = over_turns(jnp.max(scores, axis=0, keepdims=True), jnp.maximum)
    expo = jnp.exp(scores - jnp.concatenate([top, top], axis=1)[:1])
    expo_ref[...] = expo
    total = over_turns(jnp.sum(expo, axis=0, keepdims=True), jnp.add)
    for device in range(stats_ref.shape[0]):
        stats_ref[device, 0:1, :] = top[:1]
        stats_ref[device, 1:2, :] = total[:1]


def sum_kernel(first, stats_ref, mine_ref, expo_ref, weighted_ref, groups_ref, out_ref, *rest):
    scaled = rest[-1]
    tops = stats_ref[:, 0, :]
    top = jnp.max(tops, axis=0, keepdims=True)
    total = jnp.sum(stats_ref[:, 1, :] * jnp.exp(tops - top), axis=0, keepdims=True)
    for evidence_ref in rest[:-1]:
        evidence_ref[...] = (top + jnp.log(total))[:, :IMGS]
    factor = jnp.exp(mine_ref[0, 0:1, :] - top) / total
    factor = jnp.concatenate([factor, factor], axis=1)
    half = KDEV // 2
    for turn in range(TURNS):
        source = turn * KDEV + first
        value = expo_ref[source : source + half, :] * factor
        scaled[turn * half : (turn + 1) * half, :] = value.astype(bf16)
    weights = scaled[...]
    for pair in range(PAIRS):
        part = dot(weights, image_tile(weighted_ref, pair), NN)
        for turn in range(TURNS):
            to = (pair - 2 * turn) % PAIRS
            at = slice(to * 256, (to + 1) * 256)
            value = part[turn * half : (turn + 1) * half]
            if pair < 2:
                out_ref[:, at] = value
            else:
                out_ref[:, at] += value
    member = jnp.where(group_rows(groups_ref[...], STEP * GROUPS) == 0, 1.0, 0.0).astype(bf16)
    member = jnp.concatenate([member, member], axis=0)
    counts = dot(weights, member, NT)
    low = lax.broadcasted_iota(jnp.int32, (half, 128), 1) < 64
    for pair in range((TURNS + 1) // 2):
        even = counts[2 * pair * half : (2 * pair + 1) * half]
        if 2 * pair + 1 < TURNS:
            odd = counts[(2 * pair + 1) * half : (2 * pair + 2) * half]
        else:
            odd = jnp.zeros_like(even)
        out_ref[:, FULL + pair * 128 : FULL + (pair + 1) * 128] = jnp.where(low, even, odd)


def last_kernel(a_ref, b_ref, c_ref, d_ref, weight_ref, sums_ref, ctf_ref):
    total = (a_ref[...] + b_ref[...]) + (c_ref[...] + d_ref[...])
    sums_ref[...] = total[:, :FULL]
    counts = jnp.concatenate([total[:, FULL:], jnp.zeros((6, SENT - FULL), f32)], axis=0)
    low = lax.broadcasted_iota(jnp.int32, (8, 128), 1) < 64
    rows = []
    for turn in range(TURNS):
        value = counts[:, (turn // 2) * 128 : (turn // 2 + 1) * 128]
        rows.append(jnp.where(low if turn % 2 == 0 else ~low, value, 0.0))
    counts = jnp.concatenate(rows, axis=0)
    counts = jnp.concatenate([counts] * 2, axis=1)
    high = counts.astype(bf16)
    low = counts - high.astype(f32)
    counts = jnp.concatenate([high.astype(f32), low], axis=0).astype(bf16)
    size = STEP * GROUPS
    weight = jnp.concatenate(
        [weight_ref[(piece // 2) * size : (piece // 2 + 1) * size, :] for piece in range(4)], axis=0
    )
    spread = dot(counts, weight, NN)
    spread = spread[: 8 * TURNS] + spread[8 * TURNS :]
    for tile in range(TILES):
        value = None
        for turn in range(TURNS):
            source = (tile + turn) % TILES
            term = spread[turn * 8 : (turn + 1) * 8, source * 256 : (source + 1) * 256]
            value = term if value is None else value + term
        ctf_ref[:, tile * 256 : (tile + 1) * 256] = value[:2]


LIMIT = pltpu.CompilerParams(vmem_limit_bytes=48 * 1024 * 1024)


def shape(*dims, dtype=f32):
    return jax.ShapeDtypeStruct(dims, dtype)


def on_device(images, references, shifts, ctf_groups, ctf_table, noise_var):
    cls = lax.axis_size("cls")
    groups = ctf_groups.reshape(1, -1)
    inputs = (images, references, shifts.T, groups, ctf_table, noise_var.reshape(1, -1))
    inputs = tuple(pltpu.with_memory_space_constraint(v, pltpu.HBM) for v in inputs)
    expo, weighted, stats, weight, groups = pl.pallas_call(
        score_kernel,
        out_shape=(
            shape(ROWS, COLS),
            shape(IMGS, FULL, dtype=bf16),
            shape(cls, 2, 128),
            shape(2 * STEP * GROUPS, PLANE, dtype=bf16),
            shape(1, IMGS, dtype=jnp.int32),
        ),
        in_specs=[pl.BlockSpec(memory_space=pltpu.HBM)] * 6,
        scratch_shapes=[pltpu.VMEM(value.shape, value.dtype) for value in inputs]
        + [
            pltpu.VMEM((KDEV, FULL), bf16),
            pltpu.VMEM((KDEV, PLANE), bf16),
            pltpu.VMEM((KDEV, PLANE), bf16),
            pltpu.VMEM((WIDTH, PLANE), bf16),
            pltpu.VMEM((WIDTH, PLANE), bf16),
            pltpu.VMEM((IMGS, PLANE), f32),
            pltpu.VMEM((IMGS, PLANE), f32),
            pltpu.SemaphoreType.DMA((6,)),
        ],
        compiler_params=LIMIT,
        name="scores",
    )(*inputs)
    gathered = lax.all_to_all(stats, "cls", 0, 0)
    sums = []
    for first in (0, KDEV // 2):
        evidence = [shape(1, IMGS)] if first else []
        sums += pl.pallas_call(
            functools.partial(sum_kernel, first),
            out_shape=[shape(KDEV // 2, SENT)] + evidence,
            scratch_shapes=[pltpu.VMEM((ROWS // 2, COLS), bf16)],
            compiler_params=LIMIT,
            cost_estimate=pl.CostEstimate(
                flops=ROWS * COLS * FULL, bytes_accessed=2 * ROWS * COLS, transcendentals=0
            ),
            name="sums",
        )(gathered, stats, expo, weighted, groups)
    send, keep, evidence = sums

    count = lax.axis_size("img")
    over_core = [(i, i ^ 1) for i in range(count)]
    half = keep + lax.ppermute(send, "img", over_core)

    def step(value, d, stage):
        pairs = []
        for i in range(count):
            pairs.append((i, i ^ (2 * d if i % 2 == stage else 8 * d)))
        return lax.ppermute(value, "img", pairs)

    quarter = half[:8]
    for d in (2, 1, 3):
        quarter = quarter + step(half[8 * d : 8 * d + 8], d, 0)
    parts = [quarter[:2]]
    for d in (1, 3, 2):
        parts.append(step(quarter[2 * d : 2 * d + 2], d, 1))
    class_sums, ctf_sums = pl.pallas_call(
        last_kernel,
        out_shape=(shape(2, FULL), shape(2, PLANE)),
        compiler_params=LIMIT,
        name="ctf",
    )(*parts, weight)
    return class_sums, ctf_sums, evidence.reshape(-1)


def solution(mesh):
    placed = (P("img", None), P("cls", None), P("img", None), P("img"), P(), P())
    return jax.shard_map(
        on_device,
        mesh=mesh,
        in_specs=placed,
        out_specs=(P(("cls", "img"), None), P(("cls", "img"), None), P("img")),
        check_vma=False,
    )
```

```python
import functools
import math

import jax
import jax.numpy as jnp
import numpy as np
from jax import lax
from jax.experimental import pallas as pl
from jax.experimental.pallas import tpu as pltpu
from jax.sharding import PartitionSpec as P

ROT = 36
CYCLES = 32
ANG = 72
BOX = 64
GROUPS = 16
IMGS = 64
KDEV = 64
FULL = 2 * ANG * CYCLES
PLANE = ANG * CYCLES
STEP = 4
TURNS = ROT // STEP
ROWS = TURNS * KDEV
COLS = STEP * IMGS
PAIRS = FULL // 256
TILES = PLANE // 256
SENT = FULL + 640
WIDE = 12
WIDTH = 256
PARTS = 3

f32 = jnp.float32
bf16 = jnp.bfloat16
NT = (((1,), (1,)), ((), ()))
NN = (((1,), (0,)), ((), ()))


def trig_fit():
    grid = 0.5 * np.cos(np.pi * (np.arange(2000) + 0.5) / 2000)
    square = grid * grid
    cosine = np.polynomial.chebyshev.Chebyshev.fit(square, np.cos(2 * np.pi * grid), 6)
    sine = np.polynomial.chebyshev.Chebyshev.fit(square, np.sin(2 * np.pi * grid) / grid, 6)
    to_power = lambda fit: [float(c) for c in fit.convert(kind=np.polynomial.Polynomial).coef]
    return to_power(cosine), to_power(sine)


COS, SIN = trig_fit()


def horner(coefficients, x):
    value = jnp.full_like(x, coefficients[-1])
    for c in coefficients[-2::-1]:
        value = value * x + c
    return value


def split3(x):
    high = x.astype(bf16)
    rest = x - high.astype(f32)
    middle = rest.astype(bf16)
    low = (rest - middle.astype(f32)).astype(bf16)
    return high, middle, low


def dot(a, b, dims):
    return lax.dot_general(a, b, dims, preferred_element_type=f32)


def block(ref, index, count, width=256):
    index = index % count
    return ref[:, index * width : (index + 1) * width]


def image_tile(w_ref, pair):
    rows = []
    for s in range(STEP):
        first = (2 * pair + s) % (2 * PAIRS)
        if first + 1 < 2 * PAIRS:
            rows.append(w_ref[:, first * 128 : first * 128 + 256])
        else:
            rows.append(jnp.concatenate([w_ref[:, first * 128 :], w_ref[:, :128]], axis=1))
    return jnp.concatenate(rows, axis=0)


def group_rows(groups, rows):
    row = lax.broadcasted_iota(jnp.int32, (rows, COLS), 0)
    column = lax.broadcasted_iota(jnp.int32, (rows, COLS), 1)
    wide = jnp.concatenate([groups] * STEP, axis=1)
    return jnp.where((row & (GROUPS - 1)) == wide, (row >> 4) - (column >> 6), -1)


def score_kernel(
    images_hbm, references_hbm, moves_hbm, groups_hbm, ctf_hbm, noise_hbm,
    expo_ref, weighted_ref, stats_ref, weight_ref, kept_ref,
    images_ref, references_ref, moves_ref, groups_ref, ctf_ref, noise_ref,
    refs, power_high, power_low, wide_high, wide_low, cosines, sines, arrived,
):
    copies = [
        pltpu.make_async_copy(source, target, arrived.at[index])
        for index, (source, target) in enumerate(
            [
                (moves_hbm, moves_ref),
                (groups_hbm, groups_ref),
                (noise_hbm, noise_ref),
                (ctf_hbm, ctf_ref),
                (references_hbm, references_ref),
                (images_hbm, images_ref),
            ]
        )
    ]
    for copy in copies:
        copy.start()

    lane = lax.broadcasted_iota(jnp.int32, (1, 128), 1)
    lane64 = lax.broadcasted_iota(jnp.int32, (64, 128), 1)
    swap = lax.broadcasted_iota(jnp.int32, (256, 256), 0) ^ 32
    swap = swap == lax.broadcasted_iota(jnp.int32, (256, 256), 1)
    swap = jnp.where(swap, 1.0, 0.0).astype(bf16)

    place = lax.axis_index("img")
    core, x, z = lax.rem(place, 2), lax.rem(lax.div(place, 2), 4), lax.div(place, 8)
    out_row = lax.broadcasted_iota(jnp.int32, (KDEV, KDEV), 0)
    in_row = lax.broadcasted_iota(jnp.int32, (KDEV, KDEV), 1)
    to_core = jnp.where(out_row < 32, 1 - core, core)
    near, later = out_row >> 3, out_row >> 1
    to_x = x ^ (jnp.where(to_core == 0, near, later) & 3)
    to_z = z ^ (jnp.where(to_core == 0, later, near) & 3)
    order = in_row == to_z * 16 + to_x * 4 + to_core * 2 + (out_row & 1)
    order = jnp.where(order, 1.0, 0.0).astype(bf16)

    copies[0].wait()
    copies[1].wait()
    groups = groups_ref[...]
    kept_ref[...] = groups
    row = lax.broadcasted_iota(jnp.int32, (128, 128), 0)
    column = jnp.concatenate([groups, groups], axis=1)
    hot = jnp.where(((row & (GROUPS - 1)) == column) & (row < 3 * GROUPS), 1.0, 0.0)
    moves = jnp.concatenate([moves_ref[...].astype(f32)] * 2, axis=1)
    hot = jnp.where(row == 3 * GROUPS, moves[0:1], hot)
    hot = jnp.where(row == 3 * GROUPS + 1, moves[1:2], hot)
    hot = jnp.where(row == 3 * GROUPS + 2, column.astype(f32), hot)
    hot = jnp.transpose(hot)[:IMGS]
    group_column = hot[:, 3 * GROUPS + 2 : 3 * GROUPS + 3].astype(jnp.int32)
    move_x = jnp.broadcast_to(hot[:, 3 * GROUPS : 3 * GROUPS + 1], (IMGS, 128))
    move_y = jnp.broadcast_to(hot[:, 3 * GROUPS + 1 : 3 * GROUPS + 2], (IMGS, 128))
    hot = hot[:, : 3 * GROUPS].astype(bf16)
    radius = ((lane & (CYCLES - 1)) + 1).astype(f32) * jnp.where((lane & CYCLES) == 0, 1.0, -1.0)
    for chunk in range(PAIRS):
        angles = [2.0 * math.pi * a / ANG for a in (2 * chunk, 2 * chunk + 1)]
        freq_x = jnp.where(lane < 64, math.cos(angles[0]), math.cos(angles[1])) * radius
        freq_y = jnp.where(lane < 64, math.sin(angles[0]), math.sin(angles[1])) * radius
        turn = move_x * (freq_x * (1.0 / BOX)) + move_y * (freq_y * (1.0 / BOX))
        turn = turn - jnp.round(turn)
        square = turn * turn
        at = slice(chunk * 128, (chunk + 1) * 128)
        cosines[:, at] = horner(COS, square)
        sines[:, at] = horner(SIN, square) * turn

    copies[2].wait()
    copies[3].wait()
    inverse = jnp.concatenate([1.0 / noise_ref[...]] * 4, axis=1)
    plane = [ctf_ref[:, t * 128 : (t + 1) * 128] for t in range(PAIRS)]
    squared = [v * v * inverse for v in plane]
    swapped = [pltpu.roll(v, 64, 1) for v in squared]
    half = lax.broadcasted_iota(jnp.int32, (GROUPS, 128), 1) < 64
    halfway = [jnp.where(half, swapped[t], swapped[(t + 1) % PAIRS]) for t in range(PAIRS)]
    spare = jnp.zeros((WIDTH - WIDE * GROUPS, PLANE), bf16)
    wide_high[WIDE * GROUPS :, :] = spare
    wide_low[WIDE * GROUPS :, :] = spare
    mixed = lax.broadcasted_iota(jnp.int32, (GROUPS, 128), 1)
    mixed = (mixed & 31) | ((mixed & 32) << 1) | ((mixed & 64) >> 1)
    for odd, values in enumerate((squared, halfway)):
        for tile, value in enumerate(values):
            high = value.astype(bf16)
            low = (value - high.astype(f32)).astype(bf16)
            for s in range(odd, STEP, 2):
                to = (tile - s // 2) % PAIRS
                at = slice(to * 128, (to + 1) * 128)
                weight_ref[s * GROUPS : (s + 1) * GROUPS, at] = high
                weight_ref[(STEP + s) * GROUPS : (STEP + s + 1) * GROUPS, at] = low
            value = jnp.take_along_axis(value, mixed, axis=1)
            high = value.astype(bf16)
            low = (value - high.astype(f32)).astype(bf16)
            for s in range(odd, WIDE, 2):
                to = (tile - s // 2) % PAIRS
                at = slice(to * 128, (to + 1) * 128)
                wide_high[s * GROUPS : (s + 1) * GROUPS, at] = high
                wide_low[s * GROUPS : (s + 1) * GROUPS, at] = low

    copies[4].wait()
    for tile in range(PAIRS):
        at = slice(tile * 256, (tile + 1) * 256)
        value = dot(order, references_ref[:, at], NN)
        refs[:, at] = value.astype(bf16)
        value = value * value
        first, second = value[:, :128], value[:, 128:]
        first = first + pltpu.roll(first, 96, 1)
        second = second + pltpu.roll(second, 32, 1)
        value = jnp.where((lane64 & 32) == 0, first, second)
        high = value.astype(bf16)
        at = slice(tile * 128, (tile + 1) * 128)
        power_high[:, at] = high
        power_low[:, at] = (value - high.astype(f32)).astype(bf16)

    spread = lax.broadcasted_iota(jnp.int32, (GROUPS, 128), 1)
    spread = (spread >> 6) * 32 + (spread & 31)
    def weigh(pair):
        at = slice(pair * 256, (pair + 1) * 256)
        cosine, sine = cosines[:, at], sines[:, at]
        for at, sign in ((pair, 1), (pair + PAIRS // 2, -1)):
            table = plane[at] * inverse
            table = jnp.concatenate(
                [
                    jnp.take_along_axis(table, spread, axis=1),
                    jnp.take_along_axis(table, spread + 64, axis=1),
                ],
                axis=1,
            )
            scale = dot(hot, jnp.concatenate(split3(table), axis=0), NN)
            at = slice(at * 256, (at + 1) * 256)
            value = images_ref[:, at]
            other = dot(value, swap, NN) * sine
            value = value.astype(f32) * cosine
            value = value + other if sign > 0 else value - other
            weighted_ref[:, at] = (value * scale).astype(bf16)

    def spun(ref, count, by, first=0, last=None):
        last = count if last is None else last
        return jnp.concatenate(
            [
                jnp.concatenate(
                    [block(ref, t - turn * by, count) for t in range(first, last)], axis=1
                )
                for turn in range(count // by)
            ],
            axis=0,
        )

    copies[5].wait()
    by_group = None
    for part in range(PARTS):
        first, last = part * TILES // PARTS, (part + 1) * TILES // PARTS
        high = spun(power_high, TILES, 3, first, last)
        low = spun(power_low, TILES, 3, first, last)
        rows = high.shape[0]
        at = slice(first * 256, last * 256)
        both = dot(jnp.concatenate([high, low], axis=0), wide_high[:, at], NT)
        both = (both[:rows] + both[rows:]) + dot(high, wide_low[:, at], NT)
        by_group = both if by_group is None else by_group + both
        for pair in range(first, last):
            weigh(pair)

    pieces = jnp.concatenate(split3(by_group), axis=1)
    lane = lax.broadcasted_iota(jnp.int32, (KDEV, pieces.shape[1]), 1)
    third = (lane >> 6) & 3
    penalty = [
        jnp.where(third == turn % 3, pieces[turn // 3 * KDEV : (turn // 3 + 1) * KDEV], 0)
        for turn in range(TURNS)
    ]
    penalty = jnp.concatenate(penalty, axis=0).astype(bf16)
    lane = lax.broadcasted_iota(jnp.int32, (IMGS, WIDTH), 1)
    mine = ((lane & (GROUPS - 1)) == group_column) & (lane < WIDE * GROUPS)
    member = [
        jnp.where(mine & (((lane >> 4) & 3) == s), -0.5, 0.0).astype(bf16) for s in range(STEP)
    ]
    member = jnp.concatenate(member, axis=0)
    moved = [image_tile(weighted_ref, t) for t in range(PAIRS)]
    moved = jnp.concatenate(moved + [member] * 3, axis=1)
    scores = dot(jnp.concatenate([spun(refs, PAIRS, 2), penalty], axis=1), moved, NT)

    def over_turns(value, join):
        value = join(value[:, :128], value[:, 128:])
        value = jnp.broadcast_to(value, (8, 128))
        return join(value, pltpu.roll(value, 64, 1))

    top = over_turns(jnp.max(scores, axis=0, keepdims=True), jnp.maximum)
    expo = jnp.exp(scores - jnp.concatenate([top, top], axis=1)[:1])
    expo_ref[...] = expo
    total = over_turns(jnp.sum(expo, axis=0, keepdims=True), jnp.add)
    for device in range(stats_ref.shape[0]):
        stats_ref[device, 0:1, :] = top[:1]
        stats_ref[device, 1:2, :] = total[:1]


def sum_kernel(first, stats_ref, mine_ref, expo_ref, weighted_ref, groups_ref, out_ref, *rest):
    scaled = rest[-1]
    tops = stats_ref[:, 0, :]
    top = jnp.max(tops, axis=0, keepdims=True)
    total = jnp.sum(stats_ref[:, 1, :] * jnp.exp(tops - top), axis=0, keepdims=True)
    for evidence_ref in rest[:-1]:
        evidence_ref[...] = (top + jnp.log(total))[:, :IMGS]
    factor = jnp.exp(mine_ref[0, 0:1, :] - top) / total
    factor = jnp.concatenate([factor, factor], axis=1)
    half = KDEV // 2
    for turn in range(TURNS):
        source = turn * KDEV + first
        value = expo_ref[source : source + half, :] * factor
        scaled[turn * half : (turn + 1) * half, :] = value.astype(bf16)
    weights = scaled[...]
    for pair in range(PAIRS):
        part = dot(weights, image_tile(weighted_ref, pair), NN)
        for turn in range(TURNS):
            to = (pair - 2 * turn) % PAIRS
            at = slice(to * 256, (to + 1) * 256)
            value = part[turn * half : (turn + 1) * half]
            if pair < 2:
                out_ref[:, at] = value
            else:
                out_ref[:, at] += value
    member = jnp.where(group_rows(groups_ref[...], STEP * GROUPS) == 0, 1.0, 0.0).astype(bf16)
    member = jnp.concatenate([member, member], axis=0)
    counts = dot(weights, member, NT)
    low = lax.broadcasted_iota(jnp.int32, (half, 128), 1) < 64
    for pair in range((TURNS + 1) // 2):
        even = counts[2 * pair * half : (2 * pair + 1) * half]
        if 2 * pair + 1 < TURNS:
            odd = counts[(2 * pair + 1) * half : (2 * pair + 2) * half]
        else:
            odd = jnp.zeros_like(even)
        out_ref[:, FULL + pair * 128 : FULL + (pair + 1) * 128] = jnp.where(low, even, odd)


def last_kernel(a_ref, b_ref, c_ref, d_ref, weight_ref, sums_ref, ctf_ref):
    total = (a_ref[...] + b_ref[...]) + (c_ref[...] + d_ref[...])
    sums_ref[...] = total[:, :FULL]
    counts = jnp.concatenate([total[:, FULL:], jnp.zeros((6, SENT - FULL), f32)], axis=0)
    low = lax.broadcasted_iota(jnp.int32, (8, 128), 1) < 64
    rows = []
    for turn in range(TURNS):
        value = counts[:, (turn // 2) * 128 : (turn // 2 + 1) * 128]
        rows.append(jnp.where(low if turn % 2 == 0 else ~low, value, 0.0))
    counts = jnp.concatenate(rows, axis=0)
    counts = jnp.concatenate([counts] * 2, axis=1)
    high = counts.astype(bf16)
    low = counts - high.astype(f32)
    counts = jnp.concatenate([high.astype(f32), low], axis=0).astype(bf16)
    size = STEP * GROUPS
    weight = jnp.concatenate(
        [weight_ref[(piece // 2) * size : (piece // 2 + 1) * size, :] for piece in range(4)], axis=0
    )
    spread = dot(counts, weight, NN)
    spread = spread[: 8 * TURNS] + spread[8 * TURNS :]
    for tile in range(TILES):
        value = None
        for turn in range(TURNS):
            source = (tile + turn) % TILES
            term = spread[turn * 8 : (turn + 1) * 8, source * 256 : (source + 1) * 256]
            value = term if value is None else value + term
        ctf_ref[:, tile * 256 : (tile + 1) * 256] = value[:2]


LIMIT = pltpu.CompilerParams(vmem_limit_bytes=48 * 1024 * 1024)


def shape(*dims, dtype=f32):
    return jax.ShapeDtypeStruct(dims, dtype)


def on_device(images, references, shifts, ctf_groups, ctf_table, noise_var):
    cls = lax.axis_size("cls")
    groups = ctf_groups.reshape(1, -1)
    inputs = (images, references, shifts.T, groups, ctf_table, noise_var.reshape(1, -1))
    inputs = tuple(pltpu.with_memory_space_constraint(v, pltpu.HBM) for v in inputs)
    expo, weighted, stats, weight, groups = pl.pallas_call(
        score_kernel,
        out_shape=(
            shape(ROWS, COLS),
            shape(IMGS, FULL, dtype=bf16),
            shape(cls, 2, 128),
            shape(2 * STEP * GROUPS, PLANE, dtype=bf16),
            shape(1, IMGS, dtype=jnp.int32),
        ),
        in_specs=[pl.BlockSpec(memory_space=pltpu.HBM)] * 6,
        scratch_shapes=[pltpu.VMEM(value.shape, value.dtype) for value in inputs]
        + [
            pltpu.VMEM((KDEV, FULL), bf16),
            pltpu.VMEM((KDEV, PLANE), bf16),
            pltpu.VMEM((KDEV, PLANE), bf16),
            pltpu.VMEM((WIDTH, PLANE), bf16),
            pltpu.VMEM((WIDTH, PLANE), bf16),
            pltpu.VMEM((IMGS, PLANE), f32),
            pltpu.VMEM((IMGS, PLANE), f32),
            pltpu.SemaphoreType.DMA((6,)),
        ],
        compiler_params=LIMIT,
        name="scores",
    )(*inputs)
    gathered = lax.all_to_all(stats, "cls", 0, 0)
    sums = []
    for first in (0, KDEV // 2):
        evidence = [shape(1, IMGS)] if first else []
        sums += pl.pallas_call(
            functools.partial(sum_kernel, first),
            out_shape=[shape(KDEV // 2, SENT)] + evidence,
            scratch_shapes=[pltpu.VMEM((ROWS // 2, COLS), bf16)],
            compiler_params=LIMIT,
            cost_estimate=pl.CostEstimate(
                flops=ROWS * COLS * FULL, bytes_accessed=2 * ROWS * COLS, transcendentals=0
            ),
            name="sums",
        )(gathered, stats, expo, weighted, groups)
    send, keep, evidence = sums

    count = lax.axis_size("img")
    over_core = [(i, i ^ 1) for i in range(count)]
    half = keep + lax.ppermute(send, "img", over_core)

    def step(value, d, stage):
        pairs = []
        for i in range(count):
            pairs.append((i, i ^ (2 * d if i % 2 == stage else 8 * d)))
        return lax.ppermute(value, "img", pairs)

    quarter = half[:8]
    for d in (2, 1, 3):
        quarter = quarter + step(half[8 * d : 8 * d + 8], d, 0)
    parts = [quarter[:2]]
    for d in (1, 2, 3):
        parts.append(step(quarter[2 * d : 2 * d + 2], d, 1))
    class_sums, ctf_sums = pl.pallas_call(
        last_kernel,
        out_shape=(shape(2, FULL), shape(2, PLANE)),
        compiler_params=LIMIT,
        name="ctf",
    )(*parts, weight)
    return class_sums, ctf_sums, evidence.reshape(-1)


def solution(mesh):
    placed = (P("img", None), P("cls", None), P("img", None), P("img"), P(), P())
    return jax.shard_map(
        on_device,
        mesh=mesh,
        in_specs=placed,
        out_specs=(P(("cls", "img"), None), P(("cls", "img"), None), P("img")),
        check_vma=False,
    )
```
